256 devices in a mesh: lon: 4 (over x), lat: 64 (over z, y, core).
Axes of the slice: x: 4, y: 4, z: 8, core: 2. Of those that a mesh axis runs over, the one named last changes fastest.
Arguments:
- grid_latent: bfloat16 [196608, 256], P(('lon', 'lat')), may hold values from -6 to 6
- mesh_latent: bfloat16 [8192, 256], P('lon'), may hold values from -6 to 6
- edge_latent: bfloat16 [524288, 256], P(('lon', 'lat')), may hold values from -6 to 6
- mesh_cotangent: bfloat16 [8192, 256], P('lon'), may hold values from -6 to 6
- edge_senders: int32 [524288], P(('lon', 'lat')), may hold values from 0 to 191
- edge_receivers: int32 [524288], P(('lon', 'lat')), may hold values from 0 to 2047
- send_rows: int32 [256, 192], P(('lon', 'lat')), may hold values from 0 to 767
- edge_count: int32 [256], P(('lon', 'lat')), may hold values from 1 to 2048, 393216 in all
- edge_first: bfloat16 [768, 256], replicated, may hold values from -0.21875 to 0.21875
- edge_second: bfloat16 [256, 256], replicated, may hold values from -0.375 to 0.375
- edge_gain: float32 [256], replicated, may hold values from 0.5 to 1.5
- node_first: bfloat16 [512, 256], replicated, may hold values from -0.25 to 0.25
- node_second: bfloat16 [256, 256], replicated, may hold values from -0.375 to 0.375
- node_gain: float32 [256], replicated, may hold values from 0.5 to 1.5
Outputs:
- mesh_out: bfloat16 [8192, 256], P(('lon', 'lat'))
- grid_grad: bfloat16 [196608, 256], P(('lon', 'lat'))
- mesh_grad: bfloat16 [8192, 256], P(('lon', 'lat'))
- edge_grad: bfloat16 [524288, 256], P(('lon', 'lat'))
The draws below stay inside these ranges and needn't reach their ends.
Inputs may be any that keep to these rules, and one draw needn't show every extreme that they name: `edge_count`: the live slots of a block come first; some block is full.
All inputs are finite; a program needn't handle non-finite values.
Results may differ from the reference program's by a relative error of at most 0.015.
Values may be sent and summed in bfloat16 or wider, within the bound.
No kernel may reach another device: no remote copies, remote signals or barrier semaphores. Data moves between devices by JAX's collectives and lax.ppermute only.
A program may use at most 64 MiB of HBM per device.

```python
import math
import jax
import jax.numpy as jnp
import numpy as np
from jax import lax

D = 256
G_DEV = 768
E_DEV = 2048
M_DEV = 32
CAP = 64
GRID = 196608
EDGES = 524288
MESH = 8192
N_LON = 4
N_LAT = 64


def draw_edge_receivers(key, part):
    key = jax.random.fold_in(key, 7)
    near_key, far_key, pick_key = jax.random.split(key, 3)
    total = E_DEV * N_LON * N_LAT
    block = jnp.arange(total, dtype=jnp.int32) // E_DEV
    band = (block % N_LAT + N_LAT // 2) % N_LAT
    near = band * M_DEV + jax.random.randint(near_key, (total,), 0, M_DEV, dtype=jnp.int32)
    far = jax.random.randint(far_key, (total,), 0, M_DEV * N_LAT, dtype=jnp.int32)
    pick = jax.random.randint(pick_key, (total,), 0, 2, dtype=jnp.int32)
    return jnp.where(pick == 1, near, far).astype(jnp.int32)


def set_ends(result, stream_key, smallest, top_value):
    shape = result.shape
    index_at = [jax.random.randint(jax.random.fold_in(stream_key, axis), (), 0, shape[axis]) for axis in range(len(shape))]
    result = result.at[tuple(index_at)].set(smallest)
    longest = shape.index(max(shape))
    index_at[longest] = (index_at[longest] + 1) % shape[longest]
    return result.at[tuple(index_at)].set(top_value)


def block_levels(rng, dims, cuts, least, top_value):
    level, own = 1.0, jax.random.fold_in(rng, 6)
    for axis_at, shards_of in cuts:
        steps = jnp.exp(jax.random.uniform(jax.random.fold_in(own, axis_at), (shards_of,), jnp.float32, least / len(cuts), top_value / len(cuts)))
        level = level * jnp.repeat(steps, dims[axis_at] // shards_of).reshape([-1 if axis == axis_at else 1 for axis in range(len(dims))])
    return level


def length_profile(count, total, limit, lean):
    loads = [(1 << 20) // math.isqrt(standing ** lean) + 1 for standing in range(2, count + 1)]
    rest, given = total - limit - (count - 1), [1] * (count - 1)
    while rest > 0:
        candidates = [i for i in range(count - 1) if given[i] < limit]
        pool, left = sum([loads[i] for i in candidates]), rest
        for i in candidates:
            addition = min(limit - given[i], max(1, left * loads[i] // pool), rest)
            given[i] = given[i] + addition
            rest = rest - addition
    return np.array([limit] + given)


def uneven_parts(key, count, total, reach, slope):
    if count == 2:
        one = jax.random.randint(key, (), max(1, total - reach), min(reach, total - 1) + 1)
        return jnp.stack([one, total - one])
    lengths = jnp.asarray(length_profile(count, total, reach, slope), jnp.int32)
    couples = (count - 1) // 2
    source_of, taker = lengths[1:1 + 2 * couples:2], lengths[2:2 + 2 * couples:2]
    room = jnp.minimum(source_of - 1, reach - taker)
    shifted = jax.random.randint(jax.random.fold_in(key, 1), (couples,), 0, 1 << 20) % (room + 1)
    lengths = lengths.at[1:1 + 2 * couples:2].set(source_of - shifted).at[2:2 + 2 * couples:2].set(taker + shifted)
    return lengths[jax.random.permutation(jax.random.fold_in(key, 2), count)]


def scatter_about(own_key, dims, spread, limit, cuts=(), kind=jnp.bfloat16):
    array = jax.random.normal(own_key, dims, jnp.float32) * spread
    if len(cuts) > 0:
        array = block_levels(own_key, dims, cuts, -0.22, 0.18) * array
    return jnp.clip(array, min=-limit, max=limit).astype(kind)


def setup_inputs(seed: int = 0) -> dict:
    keys = jax.random.split(jax.random.key(seed), 15)
    return {
        "grid_latent": scatter_about(keys[0], (GRID, D), 1.0, 6.0, ((0, 256),)),
        "mesh_latent": scatter_about(keys[1], (MESH, D), 1.0, 6.0, ((0, 4),)),
        "edge_latent": scatter_about(keys[2], (EDGES, D), 1.0, 6.0, ((0, 256),)),
        "mesh_cotangent": scatter_about(keys[3], (MESH, D), 1.0, 6.0, ((0, 4),)),
        "edge_senders": set_ends(jax.random.randint(keys[4], (EDGES,), 0, 3 * CAP), jax.random.fold_in(keys[4], 1), 0, (3 * CAP) - 1).astype(jnp.int32),
        "edge_receivers": draw_edge_receivers(jax.random.fold_in(keys[14], 71), 0),
        "send_rows": set_ends(jax.random.randint(keys[6], (N_LON * N_LAT, 3 * CAP), 0, G_DEV), jax.random.fold_in(keys[6], 1), 0, G_DEV - 1).astype(jnp.int32),
        "edge_count": uneven_parts(keys[7], N_LON * N_LAT, 3 * E_DEV * N_LON * N_LAT // 4, E_DEV, 2).astype(jnp.int32),
        "edge_first": scatter_about(keys[8], (3 * D, D), (3 * D) ** -0.5, 0.21875),
        "edge_second": scatter_about(keys[9], (D, D), D ** -0.5, 0.375),
        "edge_gain": jnp.clip(1.0 + 0.1 * jax.random.normal(keys[10], (D,), jnp.float32), 0.5, 1.5),
        "node_first": scatter_about(keys[11], (2 * D, D), (2 * D) ** -0.5, 0.25),
        "node_second": scatter_about(keys[12], (D, D), D ** -0.5, 0.375),
        "node_gain": jnp.clip(1.0 + 0.1 * jax.random.normal(keys[13], (D,), jnp.float32), 0.5, 1.5),
    }


eps = 1e-05

def swish_grad(value):
    sigma = jax.nn.sigmoid(value)
    return sigma * (1.0 + value * (1.0 - sigma))

def norm_forward(value, gain):
    center = value - lax.optimization_barrier(jnp.mean(value, axis=-1, keepdims=True))
    factor = lax.rsqrt(lax.optimization_barrier(jnp.mean(center * center, axis=-1, keepdims=True)) + eps)
    return center * factor * gain

def norm_backward(value, gain, upstream):
    center = value - lax.optimization_barrier(jnp.mean(value, axis=-1, keepdims=True))
    factor = lax.rsqrt(lax.optimization_barrier(jnp.mean(center * center, axis=-1, keepdims=True)) + eps)
    normed = center * factor
    scaled = upstream * gain
    return factor * (scaled - lax.optimization_barrier(jnp.mean(scaled, axis=-1, keepdims=True)) - normed * lax.optimization_barrier(jnp.mean(scaled * normed, axis=-1, keepdims=True)))

def reference(grid_latent, mesh_latent, edge_latent, mesh_cotangent, edge_senders, edge_receivers, send_rows, edge_count, edge_first, edge_second, edge_gain, node_first, node_second, node_gain):
    width = D
    w_edge = edge_first[0:width]
    w_grid = edge_first[width:2 * width]
    w_mesh = edge_first[2 * width:3 * width]
    blocks = jnp.arange(N_LON * N_LAT, dtype=jnp.int32)

    def edge_forward(block):
        lon_pos = block // N_LAT
        lat_pos = block % N_LAT
        start = block * E_DEV
        edges = lax.dynamic_slice_in_dim(edge_latent, start, E_DEV, 0)
        slots = lax.dynamic_slice_in_dim(edge_senders, start, E_DEV, 0)
        offset = (slots // CAP).astype(jnp.int32)
        owner = ((lon_pos - 1 + offset) % N_LON * N_LAT + lat_pos).astype(jnp.int32)
        local_row = send_rows[owner, (2 - offset) * CAP + slots % CAP]
        sources = (owner * G_DEV + local_row).astype(jnp.int32)
        targets = (lon_pos * (M_DEV * N_LAT) + lax.dynamic_slice_in_dim(edge_receivers, start, E_DEV, 0)).astype(jnp.int32)
        source_rows = jnp.take(grid_latent, sources, axis=0)
        target_rows = jnp.take(mesh_latent, targets, axis=0)
        live = (jnp.arange(E_DEV, dtype=jnp.int32) < edge_count[block]).astype(jnp.float32)[:, None]
        first = jnp.dot(edges, w_edge, preferred_element_type=jnp.float32)
        first = first + jnp.dot(source_rows, w_grid, preferred_element_type=jnp.float32)
        first = first + jnp.dot(target_rows, w_mesh, preferred_element_type=jnp.float32)
        act = jax.nn.silu(first).astype(jnp.bfloat16)
        second = jnp.dot(act, edge_second, preferred_element_type=jnp.float32)
        return (first, second, live, sources, targets)

    def add_block(total, block):
        first, second, live, sources, targets = edge_forward(block)
        fresh = live * norm_forward(second, edge_gain)
        return (total.at[targets].add(fresh), None)
    aggregate, _ = lax.scan(add_block, jnp.zeros((mesh_latent.shape[0], width), jnp.float32), blocks)
    agg_low = aggregate.astype(jnp.bfloat16)
    node_pre = jnp.dot(mesh_latent, node_first[0:width], preferred_element_type=jnp.float32)
    node_pre = node_pre + jnp.dot(agg_low, node_first[width:2 * width], preferred_element_type=jnp.float32)
    node_act = jax.nn.silu(node_pre).astype(jnp.bfloat16)
    node_post = jnp.dot(node_act, node_second, preferred_element_type=jnp.float32)
    mesh_out = (mesh_latent.astype(jnp.float32) + norm_forward(node_post, node_gain)).astype(jnp.bfloat16)
    cotangent = mesh_cotangent.astype(jnp.float32)
    d_post = norm_backward(node_post, node_gain, cotangent).astype(jnp.bfloat16)
    d_pre = (jnp.dot(d_post, node_second.T, preferred_element_type=jnp.float32) * swish_grad(node_pre)).astype(jnp.bfloat16)
    d_agg = jnp.dot(d_pre, node_first[width:2 * width].T, preferred_element_type=jnp.float32).astype(jnp.bfloat16)
    direct = cotangent + jnp.dot(d_pre, node_first[0:width].T, preferred_element_type=jnp.float32)

    def back_block(carry, block):
        mesh_acc, grid_acc = carry
        first, second, live, sources, targets = edge_forward(block)
        upstream = live * jnp.take(d_agg, targets, axis=0).astype(jnp.float32)
        d_second = norm_backward(second, edge_gain, upstream).astype(jnp.bfloat16)
        d_first = (jnp.dot(d_second, edge_second.T, preferred_element_type=jnp.float32) * swish_grad(first)).astype(jnp.bfloat16)
        edge_part = jnp.dot(d_first, w_edge.T, preferred_element_type=jnp.float32).astype(jnp.bfloat16)
        grid_part = jnp.dot(d_first, w_grid.T, preferred_element_type=jnp.float32)
        mesh_part = jnp.dot(d_first, w_mesh.T, preferred_element_type=jnp.float32)
        return ((mesh_acc.at[targets].add(mesh_part), grid_acc.at[sources].add(grid_part)), edge_part)
    start_carry = (jnp.zeros((mesh_latent.shape[0], width), jnp.float32), jnp.zeros((grid_latent.shape[0], width), jnp.float32))
    (mesh_acc, grid_acc), edge_parts = lax.scan(back_block, start_carry, blocks)
    mesh_grad = (direct + mesh_acc).astype(jnp.bfloat16)
    grid_grad = grid_acc.astype(jnp.bfloat16)
    edge_grad = edge_parts.reshape(-1, width)
    return (mesh_out, grid_grad, mesh_grad, edge_grad)
```

```python
import jax
import jax.numpy as jnp
from jax import lax
from jax.experimental import pallas as pl
from jax.experimental.pallas import tpu as pltpu
from jax.sharding import Mesh
from jax.sharding import PartitionSpec as P

eps = 1e-05
f32 = jnp.float32
bf16 = jnp.bfloat16
i32 = jnp.int32

LANES = 128
CHUNK = 256
MIB = 1 << 20


def dot(a, b):
    return lax.dot_general(a, b, (((1,), (0,)), ((), ())), preferred_element_type=f32)


def dot_nt(a, b):
    return lax.dot_general(a, b, (((1,), (1,)), ((), ())), preferred_element_type=f32)


def dot_tn(a, b):
    return lax.dot_general(a, b, (((0,), (0,)), ((), ())), preferred_element_type=f32)


def split_dot_nt(a, b):
    high = a.astype(bf16)
    low = (a - high.astype(f32)).astype(bf16)
    return dot_nt(high, b) + dot_nt(low, b)


def one_hot(mask):
    return jnp.where(mask, 1.0, 0.0).astype(bf16)


def call(kernel, outs, args, smem=(), scratch=(), limit=48, flops=0, nbytes=0):
    specs = [
        pl.BlockSpec(memory_space=pltpu.SMEM if i in smem else pltpu.VMEM)
        for i in range(len(args))
    ]
    return pl.pallas_call(
        kernel,
        out_shape=[jax.ShapeDtypeStruct(s, d) for s, d in outs],
        in_specs=specs,
        out_specs=[pl.BlockSpec(memory_space=pltpu.VMEM) for _ in outs],
        scratch_shapes=list(scratch),
        compiler_params=pltpu.CompilerParams(vmem_limit_bytes=limit * MIB),
        cost_estimate=pl.CostEstimate(flops=flops, bytes_accessed=nbytes, transcendentals=0),
    )(*args)


def columns(rows_ref):
    return jnp.transpose(rows_ref[...])


def pair_column(cols, i):
    return jnp.concatenate([cols[:, 2 * i : 2 * i + 1], cols[:, 2 * i + 1 : 2 * i + 2]], axis=0)


def live_rows(rows_ref, count):
    rows = rows_ref[...]
    slot = lax.broadcasted_iota(i32, rows.shape, 0) * LANES + lax.broadcasted_iota(
        i32, rows.shape, 1
    )
    return jnp.where(slot < count, rows, -1)


def halo_rows_kernel(list_ref, grid_ref, low_ref, own_ref, high_ref):
    n = list_ref.shape[1]
    g = grid_ref.shape[0]
    hot = one_hot(lax.broadcasted_iota(i32, (g, n), 0) == list_ref[...])
    rows = dot_tn(hot, grid_ref[...]).astype(bf16)
    side = n // 3
    low_ref[...] = rows[0:side]
    own_ref[...] = rows[side : 2 * side]
    high_ref[...] = rows[2 * side :]


def mesh_rows_kernel(recv_ref, mesh_ref, out_ref):
    m = mesh_ref.shape[0]
    cols = columns(recv_ref)
    for i in range(out_ref.shape[0] // CHUNK):
        col = pair_column(cols, i)
        hot = one_hot(lax.broadcasted_iota(i32, (CHUNK, m), 1) == col)
        out_ref[i * CHUNK : (i + 1) * CHUNK, :] = dot(hot, mesh_ref[...]).astype(bf16)


def edge_forward_kernel(
    send_ref, edge_ref, mesh_rows_ref, low_ref, own_ref, high_ref, first_ref, second_ref,
    normed_ref, slope_ref,
):
    width = edge_ref.shape[1]
    listed = jnp.concatenate([low_ref[...], own_ref[...], high_ref[...]], axis=0)
    n = listed.shape[0]
    cols = columns(send_ref)
    for i in range(edge_ref.shape[0] // CHUNK):
        at = slice(i * CHUNK, (i + 1) * CHUNK)
        hot = one_hot(lax.broadcasted_iota(i32, (CHUNK, n), 1) == pair_column(cols, i))
        source = dot(hot, listed).astype(bf16)
        first = dot(edge_ref[at, :], first_ref[0:width, :])
        first = first + dot(source, first_ref[width : 2 * width, :])
        first = first + dot(mesh_rows_ref[at, :], first_ref[2 * width :, :])
        sigma = jax.nn.sigmoid(first)
        act = (first * sigma).astype(bf16)
        second = dot(act, second_ref[...])
        center = second - jnp.mean(second, axis=-1, keepdims=True)
        factor = lax.rsqrt(jnp.mean(center * center, axis=-1, keepdims=True) + eps)
        normed_ref[at, :] = (center * factor).astype(bf16)
        slope_ref[at, :] = (factor * (sigma * (1.0 + first * (1.0 - sigma)))).astype(bf16)


def half_row(i, core, own):
    return (i // own) * (2 * own) + core * own + i % own


def half_sum_kernel(own_rows, core_ref, count_ref, recv_ref, value_ref, out_ref):
    half = out_ref.shape[0]
    live = live_rows(recv_ref, count_ref[0])
    core = core_ref[0]
    step = CHUNK
    for j in range(half // step):
        row = half_row(
            lax.broadcasted_iota(i32, (step, LANES), 0) + j * step, core, own_rows
        )
        total = jnp.zeros((step, value_ref.shape[1]), f32)
        for i in range(value_ref.shape[0] // CHUNK):
            hot = jnp.concatenate(
                [
                    one_hot(row == live[2 * i : 2 * i + 1, :]),
                    one_hot(row == live[2 * i + 1 : 2 * i + 2, :]),
                ],
                axis=1,
            )
            total = total + dot(hot, value_ref[i * CHUNK : (i + 1) * CHUNK, :])
        out_ref[j * step : (j + 1) * step, :] = total.astype(bf16)


def norm(value):
    center = value - jnp.mean(value, axis=-1, keepdims=True)
    factor = lax.rsqrt(jnp.mean(center * center, axis=-1, keepdims=True) + eps)
    return center * factor, factor


def node_kernel(
    at_ref, parts_ref, mesh_ref, cot_ref, first_ref, second_ref, node_gain_ref, edge_gain_ref,
    out_ref, grad_ref, direct_ref,
):
    width = mesh_ref.shape[1]
    aggregate = jnp.sum(parts_ref[...].astype(f32), axis=0)
    agg_low = (aggregate * edge_gain_ref[...]).astype(bf16)
    mesh = mesh_ref[...]
    gain = node_gain_ref[...]
    pre = dot(mesh, first_ref[0:width, :]) + dot(agg_low, first_ref[width : 2 * width, :])
    sigma = jax.nn.sigmoid(pre)
    act = (pre * sigma).astype(bf16)
    post = dot(act, second_ref[...])
    normed, factor = norm(post)
    out_ref[...] = (mesh.astype(f32) + normed * gain).astype(bf16)
    cotangent = cot_ref[...].astype(f32)
    scaled = cotangent * gain
    d_post = factor * (
        scaled
        - jnp.mean(scaled, axis=-1, keepdims=True)
        - normed * jnp.mean(scaled * normed, axis=-1, keepdims=True)
    )
    d_pre = dot_nt(d_post.astype(bf16), second_ref[...]) * (sigma * (1.0 + pre * (1.0 - sigma)))
    d_pre = d_pre.astype(bf16)
    grad = dot_nt(d_pre, first_ref[width : 2 * width, :]).astype(bf16)
    grad_ref[...] = jnp.broadcast_to(grad[None], grad_ref.shape)
    direct_ref[...] = cotangent + dot_nt(d_pre, first_ref[0:width, :])


def edge_backward_kernel(
    own_rows, core_ref, count_ref, recv_ref, near_ref, far_ref, normed_ref, slope_ref, second_ref,
    gain_ref, out_ref,
):
    half = near_ref.shape[0]
    live = live_rows(recv_ref, count_ref[0])
    core = (live // own_rows) % 2
    place = (live // (2 * own_rows)) * own_rows + live % own_rows
    place = jnp.where(live < 0, -1, place + jnp.where(core == core_ref[0], 0, half))
    cols = jnp.transpose(place)
    gain = gain_ref[...]
    for i in range(out_ref.shape[0] // CHUNK):
        at = slice(i * CHUNK, (i + 1) * CHUNK)
        col = pair_column(cols, i)
        spot = lax.broadcasted_iota(i32, (CHUNK, half), 1)
        upstream = dot(one_hot(spot == col), near_ref[...])
        upstream = upstream + dot(one_hot(spot == col - half), far_ref[...])
        scaled = upstream * gain
        normed = normed_ref[at, :].astype(f32)
        inner = (
            scaled
            - jnp.mean(scaled, axis=-1, keepdims=True)
            - normed * jnp.mean(scaled * normed, axis=-1, keepdims=True)
        ).astype(bf16)
        out_ref[at, :] = (dot_nt(inner, second_ref[...]) * slope_ref[at, :].astype(f32)).astype(bf16)


def slot_sum_kernel(send_ref, d_first_ref, first_ref, low_ref, own_ref, high_ref):
    width = d_first_ref.shape[1]
    side = low_ref.shape[0]
    slots = 3 * side
    spot = lax.broadcasted_iota(i32, (slots, LANES), 0)
    total = jnp.zeros((slots, width), f32)
    for i in range(d_first_ref.shape[0] // CHUNK):
        hot = jnp.concatenate(
            [
                one_hot(spot == send_ref[2 * i : 2 * i + 1, :]),
                one_hot(spot == send_ref[2 * i + 1 : 2 * i + 2, :]),
            ],
            axis=1,
        )
        total = total + dot(hot, d_first_ref[i * CHUNK : (i + 1) * CHUNK, :])
    terms = split_dot_nt(total, first_ref[width : 2 * width, :]).astype(bf16)
    low_ref[...] = terms[0:side]
    own_ref[...] = terms[side : 2 * side]
    high_ref[...] = terms[2 * side :]


def edge_grad_kernel(d_first_ref, first_ref, out_ref):
    width = d_first_ref.shape[1]
    for i in range(out_ref.shape[0] // CHUNK):
        at = slice(i * CHUNK, (i + 1) * CHUNK)
        out_ref[at, :] = dot_nt(d_first_ref[at, :], first_ref[0:width, :]).astype(bf16)


def grid_grad_kernel(list_ref, low_ref, own_ref, high_ref, out_ref):
    terms = jnp.concatenate([low_ref[...], own_ref[...], high_ref[...]], axis=0)
    spot = lax.broadcasted_iota(i32, (out_ref.shape[0], terms.shape[0]), 0)
    out_ref[...] = dot(one_hot(spot == list_ref[...]), terms).astype(bf16)


def mesh_grad_kernel(parts_ref, direct_ref, first_ref, out_ref):
    width = direct_ref.shape[1]
    total = jnp.sum(parts_ref[...].astype(f32), axis=0)
    out_ref[...] = (
        direct_ref[...] + split_dot_nt(total, first_ref[2 * width : 3 * width, :])
    ).astype(bf16)


def ring(count, shift):
    return [(i, (i + shift) % count) for i in range(count)]


def shards(
    grid_latent,
    mesh_latent,
    edge_latent,
    mesh_cotangent,
    edge_senders,
    edge_receivers,
    send_rows,
    edge_count,
    edge_first,
    edge_second,
    edge_gain,
    node_first,
    node_second,
    node_gain,
):
    width = grid_latent.shape[1]
    zy = ("z", "y")
    lon_count = lax.axis_size("lon")
    owners = lax.axis_size("z") * lax.axis_size("y")
    core = lax.axis_index("core").astype(i32).reshape(1)
    other = 1 - core
    lat_pos = lax.axis_index(("z", "y", "core")).astype(i32).reshape(1)
    listed = send_rows.shape[1]
    side = listed // 3
    patch = mesh_latent.shape[0]
    own = patch // (2 * owners)
    half = patch // 2
    edges = edge_latent.shape[0]
    grid_rows = grid_latent.shape[0]
    recv = edge_receivers.reshape(edges // LANES, LANES)
    send = edge_senders.reshape(edges // LANES, LANES)
    swap = [(0, 1), (1, 0)]
    big = 2 * edges * patch * width
    dense = 2 * edges * width * width

    to_low, stay, to_high = call(
        halo_rows_kernel, [((side, width), bf16)] * 3, (send_rows, grid_latent),
        flops=2 * listed * grid_rows * width,
    )
    from_low = lax.ppermute(to_high, "lon", ring(lon_count, 1))
    from_high = lax.ppermute(to_low, "lon", ring(lon_count, -1))
    (mesh_rows,) = call(
        mesh_rows_kernel, [((edges, width), bf16)], (recv, mesh_latent), flops=big
    )
    normed, slope = call(
        edge_forward_kernel,
        [((edges, width), bf16)] * 2,
        (send, edge_latent, mesh_rows, from_low, stay, from_high, edge_first, edge_second),
        flops=5 * dense,
    )

    def half_sum(which, value):
        return call(
            lambda *refs: half_sum_kernel(own, *refs),
            [((half, width), bf16)],
            (which, edge_count, recv, value),
            smem=(0, 1),
            flops=big // 2,
        )[0]

    def to_owners(value):
        away = lax.ppermute(half_sum(other, value), "core", swap)
        here = half_sum(core, value)
        both = (here.astype(f32) + away.astype(f32)).astype(bf16)
        return lax.all_to_all(both.reshape(owners, own, width), zy, 0, 0, tiled=True)

    parts = to_owners(normed)

    def whole(*shape):
        return pl.BlockSpec(shape, lambda i, at: (0,) * len(shape))

    mesh_out, grad_copies, direct = pl.pallas_call(
        node_kernel,
        grid_spec=pltpu.PrefetchScalarGridSpec(
            num_scalar_prefetch=1,
            grid=(1,),
            in_specs=[
                whole(owners, own, width),
                pl.BlockSpec((own, width), lambda i, at: (at[0], 0)),
                pl.BlockSpec((own, width), lambda i, at: (at[0], 0)),
                whole(2 * width, width),
                whole(width, width),
                whole(1, width),
                whole(1, width),
            ],
            out_specs=[whole(own, width), whole(owners, own, width), whole(own, width)],
        ),
        out_shape=[
            jax.ShapeDtypeStruct((own, width), bf16),
            jax.ShapeDtypeStruct((owners, own, width), bf16),
            jax.ShapeDtypeStruct((own, width), f32),
        ],
        compiler_params=pltpu.CompilerParams(vmem_limit_bytes=32 * MIB),
    )(
        lat_pos, parts, mesh_latent, mesh_cotangent, node_first, node_second,
        node_gain.reshape(1, width), edge_gain.reshape(1, width),
    )
    near = lax.all_to_all(grad_copies, zy, 0, 0, tiled=True).reshape(half, width)
    far = lax.ppermute(near, "core", swap)
    (d_first,) = call(
        lambda *refs: edge_backward_kernel(own, *refs),
        [((edges, width), bf16)],
        (core, edge_count, recv, near, far, normed, slope, edge_second, edge_gain.reshape(1, width)),
        smem=(0, 1),
        flops=big + dense,
    )
    back_low, back_own, back_high = call(
        slot_sum_kernel, [((side, width), bf16)] * 3, (send, d_first, edge_first), flops=dense
    )
    got_low = lax.ppermute(back_high, "lon", ring(lon_count, 1))
    got_high = lax.ppermute(back_low, "lon", ring(lon_count, -1))
    mesh_parts = to_owners(d_first)
    (edge_grad,) = call(
        edge_grad_kernel, [((edges, width), bf16)], (d_first, edge_first), flops=dense
    )
    (grid_grad,) = call(
        grid_grad_kernel,
        [((grid_rows, width), bf16)],
        (send_rows, got_low, back_own, got_high),
        flops=2 * listed * grid_rows * width,
    )
    (mesh_grad,) = call(
        mesh_grad_kernel, [((own, width), bf16)], (mesh_parts, direct, edge_first)
    )
    return (mesh_out, grid_grad, mesh_grad, edge_grad)


def solution(mesh):
    fine = Mesh(mesh.devices.reshape(mesh.shape["lon"], 8, 4, 2), ("lon", "z", "y", "core"))
    every = ("lon", "z", "y", "core")
    rows = P(every, None)
    flat = P(every)
    patch = P("lon", None)
    return jax.shard_map(
        shards,
        mesh=fine,
        in_specs=(rows, patch, rows, patch, flat, flat, rows, flat) + (P(),) * 6,
        out_specs=(rows, rows, rows, rows),
        check_vma=False,
    )
```

```python
import jax
import jax.numpy as jnp
from jax import lax
from jax.experimental import pallas as pl
from jax.experimental.pallas import tpu as pltpu
from jax.sharding import Mesh
from jax.sharding import PartitionSpec as P

eps = 1e-05
f32 = jnp.float32
bf16 = jnp.bfloat16
i32 = jnp.int32

LANES = 128
CHUNK = 256
MIB = 1 << 20


def dot(a, b):
    return lax.dot_general(a, b, (((1,), (0,)), ((), ())), preferred_element_type=f32)


def dot_nt(a, b):
    return lax.dot_general(a, b, (((1,), (1,)), ((), ())), preferred_element_type=f32)


def dot_tn(a, b):
    return lax.dot_general(a, b, (((0,), (0,)), ((), ())), preferred_element_type=f32)


def split_dot_nt(a, b):
    high = a.astype(bf16)
    low = (a - high.astype(f32)).astype(bf16)
    return dot_nt(high, b) + dot_nt(low, b)


def one_hot(mask):
    return jnp.where(mask, 1.0, 0.0).astype(bf16)


def call(kernel, outs, args, smem=(), hbm=(), scratch=(), limit=16, flops=0, name=None):
    def space(i):
        if i in smem:
            return pltpu.SMEM
        return pltpu.HBM if i in hbm else pltpu.VMEM

    return pl.pallas_call(
        kernel,
        out_shape=[jax.ShapeDtypeStruct(s, d) for s, d in outs],
        in_specs=[pl.BlockSpec(memory_space=space(i)) for i in range(len(args))],
        out_specs=[pl.BlockSpec(memory_space=pltpu.VMEM) for _ in outs],
        scratch_shapes=list(scratch),
        compiler_params=pltpu.CompilerParams(vmem_limit_bytes=limit * MIB),
        cost_estimate=pl.CostEstimate(flops=flops, bytes_accessed=0, transcendentals=0),
        name=name,
    )(*args)


def column(cols, start, size):
    parts = [cols[:, j : j + 1] for j in range(start // LANES, (start + size) // LANES)]
    return parts[0] if len(parts) == 1 else jnp.concatenate(parts, axis=0)


def row_hot(spot, rows, start, size):
    parts = [one_hot(spot == rows[j : j + 1, :]) for j in range(start // LANES, (start + size) // LANES)]
    return jnp.concatenate(parts, axis=1)


def chunks(rows, size):
    return [(at, slice(at, at + size)) for at in range(0, rows, size)]


def live_rows(rows_ref, count):
    rows = rows_ref[...]
    slot = lax.broadcasted_iota(i32, rows.shape, 0) * LANES + lax.broadcasted_iota(
        i32, rows.shape, 1
    )
    return jnp.where(slot < count, rows, -1)


def halo_rows_kernel(list_ref, grid_ref, low_ref, own_ref, high_ref):
    n = list_ref.shape[1]
    g = grid_ref.shape[0]
    hot = one_hot(lax.broadcasted_iota(i32, (g, n), 0) == list_ref[...])
    rows = dot_tn(hot, grid_ref[...]).astype(bf16)
    side = n // 3
    low_ref[...] = rows[0:side]
    own_ref[...] = rows[side : 2 * side]
    high_ref[...] = rows[2 * side :]


def mesh_rows_kernel(recv_ref, mesh_ref, out_ref, own_ref):
    own = own_ref.shape[0]
    own_ref[...] = mesh_ref[pl.ds(pl.multiple_of(my_block() * own, own), own), :]
    m = mesh_ref.shape[0]
    cols = jnp.transpose(recv_ref[...])
    for start, at in chunks(out_ref.shape[0], LANES):
        hot = one_hot(lax.broadcasted_iota(i32, (LANES, m), 1) == column(cols, start, LANES))
        out_ref[at, :] = dot(hot, mesh_ref[...]).astype(bf16)


def edge_forward_kernel(
    send_ref, edge_ref, mesh_rows_ref, low_ref, own_ref, high_ref, first_ref, second_ref,
    cot_ref, node_gain_ref, edge_gain_ref, normed_ref, slope_ref, own_cot_ref, gains_ref,
    work_ref, post_ref,
):
    own = own_cot_ref.shape[0]
    own_cot_ref[...] = cot_ref[pl.ds(pl.multiple_of(my_block() * own, own), own), :]
    gains_ref[0:1, :] = node_gain_ref[...]
    gains_ref[1:2, :] = edge_gain_ref[...]
    listed = jnp.concatenate([low_ref[...], own_ref[...], high_ref[...]], axis=0)
    n = listed.shape[0]
    cols = jnp.transpose(send_ref[...])
    parts = chunks(edge_ref.shape[0], CHUNK)
    for start, at in parts:
        hot = one_hot(lax.broadcasted_iota(i32, (CHUNK, n), 1) == column(cols, start, CHUNK))
        source = dot(hot, listed).astype(bf16)
        given = jnp.concatenate([edge_ref[at, :], source, mesh_rows_ref[at, :]], axis=1)
        work_ref[at, :] = dot(given, first_ref[...])
    for _, at in parts:
        first = work_ref[at, :]
        sigma = jax.nn.sigmoid(first)
        act = first * sigma
        work_ref[at, :] = sigma + act * (1.0 - sigma)
        post_ref[at, :] = dot(act.astype(bf16), second_ref[...])
    for _, at in parts:
        normed, factor = norm(post_ref[at, :])
        normed_ref[at, :] = normed.astype(bf16)
        slope_ref[at, :] = (factor * work_ref[at, :]).astype(bf16)


def my_core():
    return lax.axis_index("core").astype(i32)


def my_block():
    return (lax.axis_index("z") * 8 + lax.axis_index("y") * 2 + lax.axis_index("core")).astype(i32)


def half_row(i, core, own):
    return (i // own) * (2 * own) + core * own + i % own


def half_rows(own, core, live, value_ref, start):
    spot = half_row(lax.broadcasted_iota(i32, (CHUNK, LANES), 0) + start, core, own)
    total = jnp.zeros((CHUNK, value_ref.shape[1]), f32)
    for begin, at in chunks(value_ref.shape[0], CHUNK):
        total = total + dot(row_hot(spot, live, begin, CHUNK), value_ref[at, :])
    return total


def half_sum_kernel(own, here, count_ref, recv_ref, value_ref, out_ref):
    live = live_rows(recv_ref, count_ref[0])
    core = my_core() if here else 1 - my_core()
    for start, at in chunks(out_ref.shape[0], CHUNK):
        out_ref[at, :] = half_rows(own, core, live, value_ref, start).astype(out_ref.dtype)


def half_total_kernel(own, count_ref, recv_ref, value_ref, begun_ref, away_ref, out_ref):
    done = begun_ref.shape[0]
    live = live_rows(recv_ref, count_ref[0])
    for start, at in chunks(out_ref.shape[0], CHUNK):
        if start < done:
            here = begun_ref[at, :]
        else:
            here = half_rows(own, my_core(), live, value_ref, start)
        out_ref[at, :] = (here + away_ref[at, :].astype(f32)).astype(bf16)


def norm(value):
    center = value - jnp.mean(value, axis=-1, keepdims=True)
    factor = lax.rsqrt(jnp.mean(center * center, axis=-1, keepdims=True) + eps)
    return center * factor, factor


def node_kernel(
    parts_ref, mesh_ref, cot_ref, first_ref, second_ref, gains_ref, out_ref, grad_ref, direct_ref,
):
    width = mesh_ref.shape[1]
    aggregate = jnp.sum(parts_ref[...].astype(f32), axis=0)
    agg_low = (aggregate * gains_ref[1:2, :]).astype(bf16)
    mesh = mesh_ref[...]
    gain = gains_ref[0:1, :]
    pre = dot(mesh, first_ref[0:width, :]) + dot(agg_low, first_ref[width : 2 * width, :])
    sigma = jax.nn.sigmoid(pre)
    act = (pre * sigma).astype(bf16)
    post = dot(act, second_ref[...])
    normed, factor = norm(post)
    out_ref[...] = (mesh.astype(f32) + normed * gain).astype(bf16)
    cotangent = cot_ref[...].astype(f32)
    scaled = cotangent * gain
    d_post = factor * (
        scaled
        - jnp.mean(scaled, axis=-1, keepdims=True)
        - normed * jnp.mean(scaled * normed, axis=-1, keepdims=True)
    )
    d_pre = dot_nt(d_post.astype(bf16), second_ref[...]) * (sigma * (1.0 + pre * (1.0 - sigma)))
    d_pre = d_pre.astype(bf16)
    grad = dot_nt(d_pre, first_ref[width : 2 * width, :]).astype(bf16)
    grad_ref[...] = jnp.broadcast_to(grad[None], grad_ref.shape)
    direct_ref[...] = cotangent + dot_nt(d_pre, first_ref[0:width, :])


def half_place(own, core, live):
    place = (live // (2 * own)) * own + live % own
    return jnp.where((live // own) % 2 == core, place, -1)


def near_rows_kernel(own, count_ref, recv_ref, near_ref, out_ref):
    half = near_ref.shape[0]
    place = half_place(own, my_core(), live_rows(recv_ref, count_ref[0]))
    cols = jnp.transpose(place)
    for start, at in chunks(out_ref.shape[0], LANES):
        hot = one_hot(lax.broadcasted_iota(i32, (LANES, half), 1) == column(cols, start, LANES))
        out_ref[at, :] = dot(hot, near_ref[...]).astype(bf16)


def edge_backward_kernel(
    own, count_ref, recv_ref, near_rows_ref, far_ref, normed_ref, slope_ref, second_ref,
    gains_ref, out_ref, work_ref,
):
    half = far_ref.shape[0]
    place = half_place(own, 1 - my_core(), live_rows(recv_ref, count_ref[0]))
    cols = jnp.transpose(place)
    for start, at in chunks(out_ref.shape[0], LANES):
        hot = one_hot(lax.broadcasted_iota(i32, (LANES, half), 1) == column(cols, start, LANES))
        work_ref[at, :] = dot(hot, far_ref[...]) + near_rows_ref[at, :].astype(f32)
    gain = gains_ref[1:2, :]
    for _, at in chunks(out_ref.shape[0], CHUNK):
        scaled = work_ref[at, :] * gain
        normed = normed_ref[at, :].astype(f32)
        inner = (
            scaled
            - jnp.mean(scaled, axis=-1, keepdims=True)
            - normed * jnp.mean(scaled * normed, axis=-1, keepdims=True)
        ).astype(bf16)
        out_ref[at, :] = (dot_nt(inner, second_ref[...]) * slope_ref[at, :].astype(f32)).astype(bf16)


def slot_sum_kernel(send_ref, d_first_ref, first_ref, low_ref, own_ref, high_ref):
    width = d_first_ref.shape[1]
    side = low_ref.shape[0]
    spot = lax.broadcasted_iota(i32, (3 * side, LANES), 0)
    total = jnp.zeros((3 * side, width), f32)
    for start, at in chunks(d_first_ref.shape[0], CHUNK):
        total = total + dot(row_hot(spot, send_ref, start, CHUNK), d_first_ref[at, :])
    terms = split_dot_nt(total, first_ref[width : 2 * width, :]).astype(bf16)
    low_ref[...] = terms[0:side]
    own_ref[...] = terms[side : 2 * side]
    high_ref[...] = terms[2 * side :]


def edge_grad_kernel(d_first_ref, first_ref, out_ref):
    width = d_first_ref.shape[1]
    for i in range(out_ref.shape[0] // CHUNK):
        at = slice(i * CHUNK, (i + 1) * CHUNK)
        out_ref[at, :] = dot_nt(d_first_ref[at, :], first_ref[0:width, :]).astype(bf16)


def grid_grad_kernel(list_ref, low_ref, own_ref, high_ref, out_ref):
    terms = jnp.concatenate([low_ref[...], own_ref[...], high_ref[...]], axis=0)
    spot = lax.broadcasted_iota(i32, (out_ref.shape[0], terms.shape[0]), 0)
    out_ref[...] = dot(one_hot(spot == list_ref[...]), terms).astype(bf16)


def mesh_grad_kernel(parts_ref, direct_ref, first_ref, out_ref):
    width = direct_ref.shape[1]
    total = jnp.sum(parts_ref[...].astype(f32), axis=0)
    out_ref[...] = (
        direct_ref[...] + split_dot_nt(total, first_ref[2 * width : 3 * width, :])
    ).astype(bf16)


def ring(count, shift):
    return [(i, (i + shift) % count) for i in range(count)]


def shards(
    grid_latent,
    mesh_latent,
    edge_latent,
    mesh_cotangent,
    edge_senders,
    edge_receivers,
    send_rows,
    edge_count,
    edge_first,
    edge_second,
    edge_gain,
    node_first,
    node_second,
    node_gain,
):
    width = grid_latent.shape[1]
    zy = ("z", "y")
    lon_count = lax.axis_size("lon")
    owners = lax.axis_size("z") * lax.axis_size("y")
    listed = send_rows.shape[1]
    side = listed // 3
    patch = mesh_latent.shape[0]
    own = patch // (2 * owners)
    half = patch // 2
    edges = edge_latent.shape[0]
    grid_rows = grid_latent.shape[0]
    recv = edge_receivers.reshape(edges // LANES, LANES)
    send = edge_senders.reshape(edges // LANES, LANES)
    swap = [(0, 1), (1, 0)]
    big = 2 * edges * patch * width
    dense = 2 * edges * width * width

    vm = pltpu.VMEM
    to_low, stay, to_high = call(
        halo_rows_kernel,
        [((side, width), bf16)] * 3,
        (send_rows, grid_latent),
        flops=2 * listed * grid_rows * width,
        name="halo_rows",
    )
    from_low = lax.ppermute(to_high, "lon", ring(lon_count, 1))
    from_high = lax.ppermute(to_low, "lon", ring(lon_count, -1))
    mesh_rows, own_mesh = call(
        mesh_rows_kernel, [((edges, width), bf16), ((own, width), bf16)], (recv, mesh_latent),
        flops=big,
        name="mesh_rows",
    )
    normed, slope, own_cot, gains = call(
        edge_forward_kernel,
        [((edges, width), bf16)] * 2 + [((own, width), bf16), ((2, width), f32)],
        (
            send, edge_latent, mesh_rows, from_low, stay, from_high, edge_first, edge_second,
            mesh_cotangent, node_gain.reshape(1, width), edge_gain.reshape(1, width),
        ),
        scratch=[vm((edges, width), f32)] * 2,
        flops=5 * dense,
        name="edge_forward",
    )

    def to_owners(value):
        shape = (half, width)
        begun = half - CHUNK
        (out,) = call(
            lambda *refs: half_sum_kernel(own, False, *refs), [(shape, bf16)],
            (edge_count, recv, value), smem=(0,), flops=big // 2, name="half_away",
        )
        away = lax.ppermute(out, "core", swap)
        (here,) = call(
            lambda *refs: half_sum_kernel(own, True, *refs), [((begun, width), f32)],
            (edge_count, recv, value), smem=(0,), flops=big // 2, name="half_here",
        )
        (both,) = call(
            lambda *refs: half_total_kernel(own, *refs), [(shape, bf16)],
            (edge_count, recv, value, here, away), smem=(0,), flops=big // 8,
            name="half_total",
        )
        return lax.all_to_all(both.reshape(owners, own, width), zy, 0, 0, tiled=True)

    parts = to_owners(normed)

    mesh_out, grad_copies, direct = call(
        node_kernel,
        [((own, width), bf16), ((owners, own, width), bf16), ((own, width), f32)],
        (parts, own_mesh, own_cot, node_first, node_second, gains),
        flops=2 * own * width * width * 7,
        name="node",
    )
    near = lax.all_to_all(grad_copies, zy, 0, 0, tiled=True).reshape(half, width)
    far = lax.ppermute(near, "core", swap)
    (near_rows,) = call(
        lambda *refs: near_rows_kernel(own, *refs), [((edges, width), bf16)],
        (edge_count, recv, near), smem=(0,), flops=big // 2, name="near_rows",
    )
    (d_first,) = call(
        lambda *refs: edge_backward_kernel(own, *refs),
        [((edges, width), bf16)],
        (
            edge_count, recv, near_rows, far, normed, slope, edge_second,
            gains,
        ),
        smem=(0,),
        scratch=[vm((edges, width), f32)],
        flops=big // 2 + dense,
        name="edge_backward",
    )
    back_low, back_own, back_high = call(
        slot_sum_kernel, [((side, width), bf16)] * 3, (send, d_first, edge_first), flops=dense, name="slot_sum"
    )
    got_low = lax.ppermute(back_high, "lon", ring(lon_count, 1))
    got_high = lax.ppermute(back_low, "lon", ring(lon_count, -1))
    mesh_parts = to_owners(d_first)
    (edge_grad,) = call(
        edge_grad_kernel, [((edges, width), bf16)], (d_first, edge_first), flops=dense, name="edge_grad"
    )
    (grid_grad,) = call(
        grid_grad_kernel,
        [((grid_rows, width), bf16)],
        (send_rows, got_low, back_own, got_high),
        flops=2 * listed * grid_rows * width,
        name="grid_grad",
    )
    (mesh_grad,) = call(
        mesh_grad_kernel, [((own, width), bf16)], (mesh_parts, direct, edge_first), name="mesh_grad"
    )
    return (mesh_out, grid_grad, mesh_grad, edge_grad)


def solution(mesh):
    fine = Mesh(mesh.devices.reshape(mesh.shape["lon"], 8, 4, 2), ("lon", "z", "y", "core"))
    every = ("lon", "z", "y", "core")
    rows = P(every, None)
    flat = P(every)
    patch = P("lon", None)
    return jax.shard_map(
        shards,
        mesh=fine,
        in_specs=(rows, patch, rows, patch, flat, flat, rows, flat) + (P(),) * 6,
        out_specs=(rows, rows, rows, rows),
        check_vma=False,
    )
```

```python
import jax
import jax.numpy as jnp
from jax import lax
from jax.experimental import pallas as pl
from jax.experimental.pallas import tpu as pltpu
from jax.sharding import Mesh
from jax.sharding import PartitionSpec as P

eps = 1e-05
f32 = jnp.float32
bf16 = jnp.bfloat16
i32 = jnp.int32

LANES = 128
CHUNK = 256
MIB = 1 << 20


def dot(a, b):
    return lax.dot_general(a, b, (((1,), (0,)), ((), ())), preferred_element_type=f32)


def dot_nt(a, b):
    return lax.dot_general(a, b, (((1,), (1,)), ((), ())), preferred_element_type=f32)


def dot_tn(a, b):
    return lax.dot_general(a, b, (((0,), (0,)), ((), ())), preferred_element_type=f32)


def split_dot_nt(a, b):
    high = a.astype(bf16)
    low = (a - high.astype(f32)).astype(bf16)
    return dot_nt(high, b) + dot_nt(low, b)


def one_hot(mask):
    return jnp.where(mask, 1.0, 0.0).astype(bf16)


def call(kernel, outs, args, smem=(), hbm=(), scratch=(), limit=16, flops=0, name=None):
    def space(i):
        if i in smem:
            return pltpu.SMEM
        return pltpu.HBM if i in hbm else pltpu.VMEM

    return pl.pallas_call(
        kernel,
        out_shape=[jax.ShapeDtypeStruct(s, d) for s, d in outs],
        in_specs=[pl.BlockSpec(memory_space=space(i)) for i in range(len(args))],
        out_specs=[pl.BlockSpec(memory_space=pltpu.VMEM) for _ in outs],
        scratch_shapes=list(scratch),
        compiler_params=pltpu.CompilerParams(vmem_limit_bytes=limit * MIB),
        cost_estimate=pl.CostEstimate(flops=flops, bytes_accessed=0, transcendentals=0),
        name=name,
    )(*args)


def column(cols, start, size):
    parts = [cols[:, j : j + 1] for j in range(start // LANES, (start + size) // LANES)]
    return parts[0] if len(parts) == 1 else jnp.concatenate(parts, axis=0)


def row_hot(spot, rows, start, size):
    parts = [one_hot(spot == rows[j : j + 1, :]) for j in range(start // LANES, (start + size) // LANES)]
    return jnp.concatenate(parts, axis=1)


def chunks(rows, size):
    return [(at, slice(at, at + size)) for at in range(0, rows, size)]


def live_rows(rows_ref, count):
    rows = rows_ref[...]
    slot = lax.broadcasted_iota(i32, rows.shape, 0) * LANES + lax.broadcasted_iota(
        i32, rows.shape, 1
    )
    return jnp.where(slot < count, rows, -1)


def halo_rows_kernel(list_ref, grid_ref, low_ref, own_ref, high_ref):
    n = list_ref.shape[1]
    g = grid_ref.shape[0]
    hot = one_hot(lax.broadcasted_iota(i32, (g, n), 0) == list_ref[...])
    rows = dot_tn(hot, grid_ref[...]).astype(bf16)
    side = n // 3
    low_ref[...] = rows[0:side]
    own_ref[...] = rows[side : 2 * side]
    high_ref[...] = rows[2 * side :]


def mesh_rows_kernel(count_ref, recv_ref, mesh_ref, out_ref, own_ref, live_ref):
    own = own_ref.shape[0]
    own_ref[...] = mesh_ref[pl.ds(pl.multiple_of(my_block() * own, own), own), :]
    m = mesh_ref.shape[0]
    live = live_rows(recv_ref, count_ref[...])
    live_ref[...] = live
    cols = jnp.transpose(live)
    for start, at in chunks(out_ref.shape[0], LANES):
        hot = one_hot(lax.broadcasted_iota(i32, (LANES, m), 1) == column(cols, start, LANES))
        out_ref[at, :] = dot(hot, mesh_ref[...]).astype(bf16)


def edge_forward_kernel(
    send_ref, edge_ref, mesh_rows_ref, low_ref, own_ref, high_ref, first_ref, second_ref,
    normed_ref, slope_ref, work_ref, post_ref,
):
    listed = jnp.concatenate([low_ref[...], own_ref[...], high_ref[...]], axis=0)
    n = listed.shape[0]
    cols = jnp.transpose(send_ref[...])
    parts = chunks(edge_ref.shape[0], CHUNK)
    for start, at in parts:
        hot = one_hot(lax.broadcasted_iota(i32, (CHUNK, n), 1) == column(cols, start, CHUNK))
        source = dot(hot, listed).astype(bf16)
        given = jnp.concatenate([edge_ref[at, :], source, mesh_rows_ref[at, :]], axis=1)
        work_ref[at, :] = dot(given, first_ref[...])
    for _, at in parts:
        first = work_ref[at, :]
        sigma = jax.nn.sigmoid(first)
        act = first * sigma
        work_ref[at, :] = sigma + act * (1.0 - sigma)
        post_ref[at, :] = dot(act.astype(bf16), second_ref[...])
    for _, at in parts:
        normed, factor = norm(post_ref[at, :])
        normed_ref[at, :] = normed.astype(bf16)
        slope_ref[at, :] = (factor * work_ref[at, :]).astype(bf16)


def my_core():
    return lax.axis_index("core").astype(i32)


def my_block():
    return (lax.axis_index("z") * 8 + lax.axis_index("y") * 2 + lax.axis_index("core")).astype(i32)


def half_row(i, core, own):
    return (i // own) * (2 * own) + core * own + i % own


def half_rows(own, core, live, value_ref, start):
    spot = half_row(lax.broadcasted_iota(i32, (CHUNK, LANES), 0) + start, core, own)
    total = jnp.zeros((CHUNK, value_ref.shape[1]), f32)
    for begin, at in chunks(value_ref.shape[0], CHUNK):
        total = total + dot(row_hot(spot, live, begin, CHUNK), value_ref[at, :])
    return total


def half_sum_kernel(own, here, live_ref, value_ref, out_ref):
    live = live_ref[...]
    core = my_core() if here else 1 - my_core()
    for start, at in chunks(out_ref.shape[0], CHUNK):
        out_ref[at, :] = half_rows(own, core, live, value_ref, start).astype(out_ref.dtype)


def half_total_kernel(own, live_ref, value_ref, begun_ref, away_ref, out_ref):
    done = begun_ref.shape[0]
    live = live_ref[...]
    for start, at in chunks(out_ref.shape[0], CHUNK):
        if start < done:
            here = begun_ref[at, :]
        else:
            here = half_rows(own, my_core(), live, value_ref, start)
        out_ref[at, :] = (here + away_ref[at, :].astype(f32)).astype(bf16)


def half_first_kernel(
    own, live_ref, value_ref, cot_ref, node_gain_ref, edge_gain_ref, out_ref, own_cot_ref, gains_ref
):
    half_sum_kernel(own, True, live_ref, value_ref, out_ref)
    own_cot_ref[...] = cot_ref[pl.ds(pl.multiple_of(my_block() * own, own), own), :]
    gains_ref[0:1, :] = node_gain_ref[...]
    gains_ref[1:2, :] = edge_gain_ref[...]


def norm(value):
    center = value - jnp.mean(value, axis=-1, keepdims=True)
    factor = lax.rsqrt(jnp.mean(center * center, axis=-1, keepdims=True) + eps)
    return center * factor, factor


def node_kernel(
    parts_ref, mesh_ref, cot_ref, first_ref, second_ref, gains_ref, out_ref, grad_ref, direct_ref,
):
    width = mesh_ref.shape[1]
    aggregate = jnp.sum(parts_ref[...].astype(f32), axis=0)
    agg_low = (aggregate * gains_ref[1:2, :]).astype(bf16)
    mesh = mesh_ref[...]
    gain = gains_ref[0:1, :]
    pre = dot(mesh, first_ref[0:width, :]) + dot(agg_low, first_ref[width : 2 * width, :])
    sigma = jax.nn.sigmoid(pre)
    act = (pre * sigma).astype(bf16)
    post = dot(act, second_ref[...])
    normed, factor = norm(post)
    out_ref[...] = (mesh.astype(f32) + normed * gain).astype(bf16)
    cotangent = cot_ref[...].astype(f32)
    scaled = cotangent * gain
    d_post = factor * (
        scaled
        - jnp.mean(scaled, axis=-1, keepdims=True)
        - normed * jnp.mean(scaled * normed, axis=-1, keepdims=True)
    )
    d_pre = dot_nt(d_post.astype(bf16), second_ref[...]) * (sigma * (1.0 + pre * (1.0 - sigma)))
    d_pre = d_pre.astype(bf16)
    grad = dot_nt(d_pre, first_ref[width : 2 * width, :]).astype(bf16)
    grad_ref[...] = jnp.broadcast_to(grad[None], grad_ref.shape)
    direct_ref[...] = cotangent + dot_nt(d_pre, first_ref[0:width, :])


def half_place(own, core, live):
    place = (live // (2 * own)) * own + live % own
    return jnp.where((live // own) % 2 == core, place, -1)


def near_rows_kernel(own, live_ref, near_ref, out_ref):
    half = near_ref.shape[0]
    place = half_place(own, my_core(), live_ref[...])
    cols = jnp.transpose(place)
    for start, at in chunks(out_ref.shape[0], LANES):
        hot = one_hot(lax.broadcasted_iota(i32, (LANES, half), 1) == column(cols, start, LANES))
        out_ref[at, :] = dot(hot, near_ref[...]).astype(bf16)


def edge_backward_kernel(
    own, live_ref, near_rows_ref, far_ref, normed_ref, slope_ref, second_ref,
    gains_ref, out_ref, work_ref,
):
    half = far_ref.shape[0]
    place = half_place(own, 1 - my_core(), live_ref[...])
    cols = jnp.transpose(place)
    for start, at in chunks(out_ref.shape[0], LANES):
        hot = one_hot(lax.broadcasted_iota(i32, (LANES, half), 1) == column(cols, start, LANES))
        work_ref[at, :] = dot(hot, far_ref[...]) + near_rows_ref[at, :].astype(f32)
    gain = gains_ref[1:2, :]
    for _, at in chunks(out_ref.shape[0], CHUNK):
        scaled = work_ref[at, :] * gain
        normed = normed_ref[at, :].astype(f32)
        inner = (
            scaled
            - jnp.mean(scaled, axis=-1, keepdims=True)
            - normed * jnp.mean(scaled * normed, axis=-1, keepdims=True)
        ).astype(bf16)
        out_ref[at, :] = (dot_nt(inner, second_ref[...]) * slope_ref[at, :].astype(f32)).astype(bf16)


def slot_sum_kernel(send_ref, d_first_ref, first_ref, low_ref, own_ref, high_ref):
    width = d_first_ref.shape[1]
    side = low_ref.shape[0]
    spot = lax.broadcasted_iota(i32, (3 * side, LANES), 0)
    total = jnp.zeros((3 * side, width), f32)
    for start, at in chunks(d_first_ref.shape[0], CHUNK):
        total = total + dot(row_hot(spot, send_ref, start, CHUNK), d_first_ref[at, :])
    terms = split_dot_nt(total, first_ref[width : 2 * width, :]).astype(bf16)
    low_ref[...] = terms[0:side]
    own_ref[...] = terms[side : 2 * side]
    high_ref[...] = terms[2 * side :]


def edge_grad_kernel(d_first_ref, first_ref, out_ref):
    width = d_first_ref.shape[1]
    for i in range(out_ref.shape[0] // CHUNK):
        at = slice(i * CHUNK, (i + 1) * CHUNK)
        out_ref[at, :] = dot_nt(d_first_ref[at, :], first_ref[0:width, :]).astype(bf16)


def grid_grad_kernel(list_ref, low_ref, own_ref, high_ref, out_ref):
    terms = jnp.concatenate([low_ref[...], own_ref[...], high_ref[...]], axis=0)
    spot = lax.broadcasted_iota(i32, (out_ref.shape[0], terms.shape[0]), 0)
    out_ref[...] = dot(one_hot(spot == list_ref[...]), terms).astype(bf16)


def mesh_grad_kernel(parts_ref, direct_ref, first_ref, out_ref):
    width = direct_ref.shape[1]
    total = jnp.sum(parts_ref[...].astype(f32), axis=0)
    out_ref[...] = (
        direct_ref[...] + split_dot_nt(total, first_ref[2 * width : 3 * width, :])
    ).astype(bf16)


def ring(count, shift):
    return [(i, (i + shift) % count) for i in range(count)]


def shards(
    grid_latent,
    mesh_latent,
    edge_latent,
    mesh_cotangent,
    edge_senders,
    edge_receivers,
    send_rows,
    edge_count,
    edge_first,
    edge_second,
    edge_gain,
    node_first,
    node_second,
    node_gain,
):
    width = grid_latent.shape[1]
    zy = ("z", "y")
    lon_count = lax.axis_size("lon")
    owners = lax.axis_size("z") * lax.axis_size("y")
    listed = send_rows.shape[1]
    side = listed // 3
    patch = mesh_latent.shape[0]
    own = patch // (2 * owners)
    half = patch // 2
    edges = edge_latent.shape[0]
    grid_rows = grid_latent.shape[0]
    recv = edge_receivers.reshape(edges // LANES, LANES)
    send = edge_senders.reshape(edges // LANES, LANES)
    swap = [(0, 1), (1, 0)]
    big = 2 * edges * patch * width
    dense = 2 * edges * width * width

    vm = pltpu.VMEM
    to_low, stay, to_high = call(
        halo_rows_kernel,
        [((side, width), bf16)] * 3,
        (send_rows, grid_latent),
        flops=2 * big,
        name="halo_rows",
    )
    from_low = lax.ppermute(to_high, "lon", ring(lon_count, 1))
    from_high = lax.ppermute(to_low, "lon", ring(lon_count, -1))
    mesh_rows, own_mesh, live = call(
        mesh_rows_kernel,
        [((edges, width), bf16), ((own, width), bf16), (recv.shape, i32)],
        (edge_count.reshape(1, 1), recv, mesh_latent),
        flops=big,
        name="mesh_rows",
    )
    normed, slope = call(
        edge_forward_kernel,
        [((edges, width), bf16)] * 2,
        (send, edge_latent, mesh_rows, from_low, stay, from_high, edge_first, edge_second),
        scratch=[vm((edges, width), f32)] * 2,
        flops=5 * dense,
        name="edge_forward",
    )

    def to_owners(value, extras=(), extra_outs=()):
        shape = (half, width)
        begun = half - CHUNK
        (out,) = call(
            lambda *refs: half_sum_kernel(own, False, *refs), [(shape, bf16)],
            (live, value), flops=big // 2, name="half_away",
        )
        away = lax.ppermute(out, "core", swap)
        here = call(
            (lambda *refs: half_first_kernel(own, *refs))
            if extras
            else (lambda *refs: half_sum_kernel(own, True, *refs)),
            [((begun, width), f32)] + list(extra_outs),
            (live, value) + tuple(extras), flops=big // 2, name="half_here",
        )
        (both,) = call(
            lambda *refs: half_total_kernel(own, *refs), [(shape, bf16)],
            (live, value, here[0], away), flops=big // 8, name="half_total",
        )
        parts = lax.all_to_all(both.reshape(owners, own, width), zy, 0, 0, tiled=True)
        return (parts,) + tuple(here[1:])

    parts, own_cot, gains = to_owners(
        normed,
        (mesh_cotangent, node_gain.reshape(1, width), edge_gain.reshape(1, width)),
        (((own, width), bf16), ((2, width), f32)),
    )
    mesh_out, grad_copies, direct = call(
        node_kernel,
        [((own, width), bf16), ((owners, own, width), bf16), ((own, width), f32)],
        (parts, own_mesh, own_cot, node_first, node_second, gains),
        flops=2 * own * width * width * 7,
        name="node",
    )
    near = lax.all_to_all(grad_copies, zy, 0, 0, tiled=True).reshape(half, width)
    far = lax.ppermute(near, "core", swap)
    (near_rows,) = call(
        lambda *refs: near_rows_kernel(own, *refs), [((edges, width), bf16)],
        (live, near), flops=big // 2, name="near_rows",
    )
    (d_first,) = call(
        lambda *refs: edge_backward_kernel(own, *refs),
        [((edges, width), bf16)],
        (
            live, near_rows, far, normed, slope, edge_second,
            gains,
        ),
        scratch=[vm((edges, width), f32)],
        flops=big // 2 + dense,
        name="edge_backward",
    )
    back_low, back_own, back_high = call(
        slot_sum_kernel, [((side, width), bf16)] * 3, (send, d_first, edge_first), flops=dense, name="slot_sum"
    )
    got_low = lax.ppermute(back_high, "lon", ring(lon_count, 1))
    got_high = lax.ppermute(back_low, "lon", ring(lon_count, -1))
    (mesh_parts,) = to_owners(d_first)
    (edge_grad,) = call(
        edge_grad_kernel, [((edges, width), bf16)], (d_first, edge_first), flops=dense, name="edge_grad"
    )
    (grid_grad,) = call(
        grid_grad_kernel,
        [((grid_rows, width), bf16)],
        (send_rows, got_low, back_own, got_high),
        flops=2 * listed * grid_rows * width,
        name="grid_grad",
    )
    (mesh_grad,) = call(
        mesh_grad_kernel, [((own, width), bf16)], (mesh_parts, direct, edge_first), name="mesh_grad"
    )
    return (mesh_out, grid_grad, mesh_grad, edge_grad)


def solution(mesh):
    fine = Mesh(mesh.devices.reshape(mesh.shape["lon"], 8, 4, 2), ("lon", "z", "y", "core"))
    every = ("lon", "z", "y", "core")
    rows = P(every, None)
    flat = P(every)
    patch = P("lon", None)
    return jax.shard_map(
        shards,
        mesh=fine,
        in_specs=(rows, patch, rows, patch, flat, flat, rows, flat) + (P(),) * 6,
        out_specs=(rows, rows, rows, rows),
        check_vma=False,
    )
```

```python
import jax
import jax.numpy as jnp
from jax import lax
from jax.experimental import pallas as pl
from jax.experimental.pallas import tpu as pltpu
from jax.sharding import Mesh
from jax.sharding import PartitionSpec as P

eps = 1e-05
f32 = jnp.float32
bf16 = jnp.bfloat16
i32 = jnp.int32

LANES = 128
CHUNK = 256
MIB = 1 << 20


def dot(a, b):
    return lax.dot_general(a, b, (((1,), (0,)), ((), ())), preferred_element_type=f32)


def dot_nt(a, b):
    return lax.dot_general(a, b, (((1,), (1,)), ((), ())), preferred_element_type=f32)


def dot_tn(a, b):
    return lax.dot_general(a, b, (((0,), (0,)), ((), ())), preferred_element_type=f32)


def split_dot_nt(a, b):
    high = a.astype(bf16)
    low = (a - high.astype(f32)).astype(bf16)
    return dot_nt(high, b) + dot_nt(low, b)


def one_hot(mask):
    return jnp.where(mask, 1.0, 0.0).astype(bf16)


def call(kernel, outs, args, smem=(), hbm=(), scratch=(), limit=16, flops=0, name=None):
    def space(i):
        if i in smem:
            return pltpu.SMEM
        return pltpu.HBM if i in hbm else pltpu.VMEM

    return pl.pallas_call(
        kernel,
        out_shape=[jax.ShapeDtypeStruct(s, d) for s, d in outs],
        in_specs=[pl.BlockSpec(memory_space=space(i)) for i in range(len(args))],
        out_specs=[pl.BlockSpec(memory_space=pltpu.VMEM) for _ in outs],
        scratch_shapes=list(scratch),
        compiler_params=pltpu.CompilerParams(vmem_limit_bytes=limit * MIB),
        cost_estimate=pl.CostEstimate(flops=flops, bytes_accessed=0, transcendentals=0),
        name=name,
    )(*args)


def column(cols, start, size):
    parts = [cols[:, j : j + 1] for j in range(start // LANES, (start + size) // LANES)]
    return parts[0] if len(parts) == 1 else jnp.concatenate(parts, axis=0)


def row_hot(spot, rows, start, size):
    parts = [one_hot(spot == rows[j : j + 1, :]) for j in range(start // LANES, (start + size) // LANES)]
    return jnp.concatenate(parts, axis=1)


def chunks(rows, size):
    return [(at, slice(at, at + size)) for at in range(0, rows, size)]


def live_rows(rows_ref, count):
    rows = rows_ref[...]
    slot = lax.broadcasted_iota(i32, rows.shape, 0) * LANES + lax.broadcasted_iota(
        i32, rows.shape, 1
    )
    return jnp.where(slot < count, rows, -1)


def halo_rows_kernel(list_ref, grid_ref, low_ref, own_ref, high_ref):
    n = list_ref.shape[1]
    g = grid_ref.shape[0]
    hot = one_hot(lax.broadcasted_iota(i32, (g, n), 0) == list_ref[...])
    rows = dot_tn(hot, grid_ref[...]).astype(bf16)
    side = n // 3
    low_ref[...] = rows[0:side]
    own_ref[...] = rows[side : 2 * side]
    high_ref[...] = rows[2 * side :]


def mesh_rows_kernel(count_ref, recv_ref, mesh_ref, out_ref, own_ref, live_ref):
    own = own_ref.shape[0]
    own_ref[...] = mesh_ref[pl.ds(pl.multiple_of(my_block() * own, own), own), :]
    m = mesh_ref.shape[0]
    live = live_rows(recv_ref, count_ref[...])
    live_ref[...] = live
    cols = jnp.transpose(live)
    for start, at in chunks(out_ref.shape[0], LANES):
        hot = one_hot(lax.broadcasted_iota(i32, (LANES, m), 1) == column(cols, start, LANES))
        out_ref[at, :] = dot(hot, mesh_ref[...]).astype(bf16)


def edge_forward_kernel(
    send_ref, edge_ref, mesh_rows_ref, low_ref, own_ref, high_ref, first_ref, second_ref,
    normed_ref, slope_ref, work_ref, post_ref,
):
    listed = jnp.concatenate([low_ref[...], own_ref[...], high_ref[...]], axis=0)
    n = listed.shape[0]
    cols = jnp.transpose(send_ref[...])
    parts = chunks(edge_ref.shape[0], CHUNK)
    for start, at in parts:
        hot = one_hot(lax.broadcasted_iota(i32, (CHUNK, n), 1) == column(cols, start, CHUNK))
        source = dot(hot, listed).astype(bf16)
        given = jnp.concatenate([edge_ref[at, :], source, mesh_rows_ref[at, :]], axis=1)
        work_ref[at, :] = dot(given, first_ref[...])
    for _, at in parts:
        first = work_ref[at, :]
        sigma = jax.nn.sigmoid(first)
        act = first * sigma
        work_ref[at, :] = sigma + act * (1.0 - sigma)
        post_ref[at, :] = dot(act.astype(bf16), second_ref[...])
    for _, at in parts:
        normed, factor = norm(post_ref[at, :])
        normed_ref[at, :] = normed.astype(bf16)
        slope_ref[at, :] = (factor * work_ref[at, :]).astype(bf16)


def my_core():
    return lax.axis_index("core").astype(i32)


def my_block():
    return (lax.axis_index("z") * 8 + lax.axis_index("y") * 2 + lax.axis_index("core")).astype(i32)


def my_lane(shift):
    return lax.rem(lax.axis_index("y").astype(i32) + shift, lax.axis_size("y"))


def block_sum(own, y, core, live, value_ref):
    lanes = lax.axis_size("y")
    i = lax.broadcasted_iota(i32, (own * lax.axis_size("z"), LANES), 0)
    spot = (i // own) * (2 * lanes * own) + (2 * y + core) * own + i % own
    total = jnp.zeros((spot.shape[0], value_ref.shape[1]), f32)
    for begin, at in chunks(value_ref.shape[0], CHUNK):
        total = total + dot(row_hot(spot, live, begin, CHUNK), value_ref[at, :])
    return total


SHIFTS = (2, 1, 3, 0)


def half_sum_kernel(own, here, live_ref, value_ref, out_ref):
    live = live_ref[...]
    core = my_core() if here else 1 - my_core()
    size = out_ref.shape[0] // len(SHIFTS)
    for n, shift in enumerate(SHIFTS):
        total = block_sum(own, my_lane(shift), core, live, value_ref)
        out_ref[n * size : (n + 1) * size, :] = total.astype(out_ref.dtype)


def half_first_kernel(
    own, live_ref, value_ref, cot_ref, node_gain_ref, edge_gain_ref, out_ref, own_cot_ref, gains_ref
):
    half_sum_kernel(own, True, live_ref, value_ref, out_ref)
    own_cot_ref[...] = cot_ref[pl.ds(pl.multiple_of(my_block() * own, own), own), :]
    gains_ref[0:1, :] = node_gain_ref[...]
    gains_ref[1:2, :] = edge_gain_ref[...]


def pieces_kernel(here_ref, away_ref, *out_refs):
    size = here_ref.shape[0] // len(out_refs)
    for n, out_ref in enumerate(out_refs):
        at = slice(n * size, (n + 1) * size)
        out_ref[...] = (here_ref[at, :] + away_ref[at, :].astype(f32)).astype(out_ref.dtype)


def total_kernel(a_ref, b_ref, c_ref, here_ref, out_ref):
    far = a_ref[...].astype(f32) + (b_ref[...].astype(f32) + c_ref[...].astype(f32))
    out_ref[...] = (here_ref[...] + far).astype(bf16).reshape(out_ref.shape)


def norm(value):
    center = value - jnp.mean(value, axis=-1, keepdims=True)
    factor = lax.rsqrt(jnp.mean(center * center, axis=-1, keepdims=True) + eps)
    return center * factor, factor


def node_kernel(
    parts_ref, mesh_ref, cot_ref, first_ref, second_ref, gains_ref, out_ref, grad_ref, direct_ref,
):
    width = mesh_ref.shape[1]
    aggregate = jnp.sum(parts_ref[...].astype(f32), axis=0)
    agg_low = (aggregate * gains_ref[1:2, :]).astype(bf16)
    mesh = mesh_ref[...]
    gain = gains_ref[0:1, :]
    pre = dot(mesh, first_ref[0:width, :]) + dot(agg_low, first_ref[width : 2 * width, :])
    sigma = jax.nn.sigmoid(pre)
    act = (pre * sigma).astype(bf16)
    post = dot(act, second_ref[...])
    normed, factor = norm(post)
    out_ref[...] = (mesh.astype(f32) + normed * gain).astype(bf16)
    cotangent = cot_ref[...].astype(f32)
    scaled = cotangent * gain
    d_post = factor * (
        scaled
        - jnp.mean(scaled, axis=-1, keepdims=True)
        - normed * jnp.mean(scaled * normed, axis=-1, keepdims=True)
    )
    d_pre = dot_nt(d_post.astype(bf16), second_ref[...]) * (sigma * (1.0 + pre * (1.0 - sigma)))
    d_pre = d_pre.astype(bf16)
    grad = dot_nt(d_pre, first_ref[width : 2 * width, :]).astype(bf16)
    grad_ref[...] = jnp.broadcast_to(grad[None], grad_ref.shape)
    direct_ref[...] = cotangent + dot_nt(d_pre, first_ref[0:width, :])


def half_place(own, core, live):
    place = (live // (2 * own)) * own + live % own
    return jnp.where((live // own) % 2 == core, place, -1)


def near_rows_kernel(own, live_ref, near_ref, out_ref):
    half = near_ref.shape[0]
    place = half_place(own, my_core(), live_ref[...])
    cols = jnp.transpose(place)
    for start, at in chunks(out_ref.shape[0], LANES):
        hot = one_hot(lax.broadcasted_iota(i32, (LANES, half), 1) == column(cols, start, LANES))
        out_ref[at, :] = dot(hot, near_ref[...]).astype(bf16)


def edge_backward_kernel(
    own, live_ref, near_rows_ref, far_ref, normed_ref, slope_ref, second_ref,
    gains_ref, out_ref, work_ref,
):
    half = far_ref.shape[0]
    place = half_place(own, 1 - my_core(), live_ref[...])
    cols = jnp.transpose(place)
    for start, at in chunks(out_ref.shape[0], LANES):
        hot = one_hot(lax.broadcasted_iota(i32, (LANES, half), 1) == column(cols, start, LANES))
        work_ref[at, :] = dot(hot, far_ref[...]) + near_rows_ref[at, :].astype(f32)
    gain = gains_ref[1:2, :]
    for _, at in chunks(out_ref.shape[0], CHUNK):
        scaled = work_ref[at, :] * gain
        normed = normed_ref[at, :].astype(f32)
        inner = (
            scaled
            - jnp.mean(scaled, axis=-1, keepdims=True)
            - normed * jnp.mean(scaled * normed, axis=-1, keepdims=True)
        ).astype(bf16)
        out_ref[at, :] = (dot_nt(inner, second_ref[...]) * slope_ref[at, :].astype(f32)).astype(bf16)


def slot_sum_kernel(send_ref, d_first_ref, first_ref, low_ref, own_ref, high_ref):
    width = d_first_ref.shape[1]
    side = low_ref.shape[0]
    spot = lax.broadcasted_iota(i32, (3 * side, LANES), 0)
    total = jnp.zeros((3 * side, width), f32)
    for start, at in chunks(d_first_ref.shape[0], CHUNK):
        total = total + dot(row_hot(spot, send_ref, start, CHUNK), d_first_ref[at, :])
    terms = split_dot_nt(total, first_ref[width : 2 * width, :]).astype(bf16)
    low_ref[...] = terms[0:side]
    own_ref[...] = terms[side : 2 * side]
    high_ref[...] = terms[2 * side :]


def edge_grad_kernel(d_first_ref, first_ref, out_ref):
    width = d_first_ref.shape[1]
    for i in range(out_ref.shape[0] // CHUNK):
        at = slice(i * CHUNK, (i + 1) * CHUNK)
        out_ref[at, :] = dot_nt(d_first_ref[at, :], first_ref[0:width, :]).astype(bf16)


def grid_grad_kernel(list_ref, low_ref, own_ref, high_ref, out_ref):
    terms = jnp.concatenate([low_ref[...], own_ref[...], high_ref[...]], axis=0)
    spot = lax.broadcasted_iota(i32, (out_ref.shape[0], terms.shape[0]), 0)
    out_ref[...] = dot(one_hot(spot == list_ref[...]), terms).astype(bf16)


def mesh_grad_kernel(parts_ref, direct_ref, first_ref, out_ref):
    width = direct_ref.shape[1]
    total = jnp.sum(parts_ref[...].astype(f32), axis=0)
    out_ref[...] = (
        direct_ref[...] + split_dot_nt(total, first_ref[2 * width : 3 * width, :])
    ).astype(bf16)


def ring(count, shift):
    return [(i, (i + shift) % count) for i in range(count)]


def shards(
    grid_latent,
    mesh_latent,
    edge_latent,
    mesh_cotangent,
    edge_senders,
    edge_receivers,
    send_rows,
    edge_count,
    edge_first,
    edge_second,
    edge_gain,
    node_first,
    node_second,
    node_gain,
):
    width = grid_latent.shape[1]
    zy = ("z", "y")
    lon_count = lax.axis_size("lon")
    owners = lax.axis_size("z") * lax.axis_size("y")
    listed = send_rows.shape[1]
    side = listed // 3
    patch = mesh_latent.shape[0]
    own = patch // (2 * owners)
    half = patch // 2
    edges = edge_latent.shape[0]
    grid_rows = grid_latent.shape[0]
    recv = edge_receivers.reshape(edges // LANES, LANES)
    send = edge_senders.reshape(edges // LANES, LANES)
    swap = [(0, 1), (1, 0)]
    big = 2 * edges * patch * width
    dense = 2 * edges * width * width

    vm = pltpu.VMEM
    to_low, stay, to_high = call(
        halo_rows_kernel,
        [((side, width), bf16)] * 3,
        (send_rows, grid_latent),
        flops=2 * big,
        name="halo_rows",
    )
    from_low = lax.ppermute(to_high, "lon", ring(lon_count, 1))
    from_high = lax.ppermute(to_low, "lon", ring(lon_count, -1))
    mesh_rows, own_mesh, live = call(
        mesh_rows_kernel,
        [((edges, width), bf16), ((own, width), bf16), (recv.shape, i32)],
        (edge_count.reshape(1, 1), recv, mesh_latent),
        flops=big,
        name="mesh_rows",
    )
    normed, slope = call(
        edge_forward_kernel,
        [((edges, width), bf16)] * 2,
        (send, edge_latent, mesh_rows, from_low, stay, from_high, edge_first, edge_second),
        scratch=[vm((edges, width), f32)] * 2,
        flops=5 * dense,
        name="edge_forward",
    )

    lanes = lax.axis_size("y")
    columns = lax.axis_size("z")
    piece = columns * own

    def to_owners(value, extras=(), extra_outs=()):
        (out,) = call(
            lambda *refs: half_sum_kernel(own, False, *refs), [((half, width), bf16)],
            (live, value), flops=big // 2, name="half_away",
        )
        away = lax.ppermute(out, "core", swap)
        here = call(
            (lambda *refs: half_first_kernel(own, *refs))
            if extras
            else (lambda *refs: half_sum_kernel(own, True, *refs)),
            [((half, width), f32)] + list(extra_outs),
            (live, value) + tuple(extras), flops=big // 2, name="half_here",
        )
        sums = call(
            pieces_kernel,
            [((piece, width), bf16 if shift else f32) for shift in SHIFTS],
            (here[0], away), name="pieces",
        )
        got = [
            lax.ppermute(total, "y", ring(lanes, shift)) if shift else total
            for shift, total in zip(SHIFTS, sums)
        ]
        (both,) = call(total_kernel, [((columns, own, width), bf16)], got, name="total")
        parts = lax.all_to_all(both, "z", 0, 0, tiled=True)
        return (parts,) + tuple(here[1:])

    parts, own_cot, gains = to_owners(
        normed,
        (mesh_cotangent, node_gain.reshape(1, width), edge_gain.reshape(1, width)),
        (((own, width), bf16), ((2, width), f32)),
    )
    mesh_out, grad_copies, direct = call(
        node_kernel,
        [((own, width), bf16), ((owners, own, width), bf16), ((own, width), f32)],
        (parts, own_mesh, own_cot, node_first, node_second, gains),
        flops=2 * own * width * width * 7,
        name="node",
    )
    near = lax.all_to_all(grad_copies, zy, 0, 0, tiled=True).reshape(half, width)
    far = lax.ppermute(near, "core", swap)
    (near_rows,) = call(
        lambda *refs: near_rows_kernel(own, *refs), [((edges, width), bf16)],
        (live, near), flops=big // 2, name="near_rows",
    )
    (d_first,) = call(
        lambda *refs: edge_backward_kernel(own, *refs),
        [((edges, width), bf16)],
        (
            live, near_rows, far, normed, slope, edge_second,
            gains,
        ),
        scratch=[vm((edges, width), f32)],
        flops=big // 2 + dense,
        name="edge_backward",
    )
    back_low, back_own, back_high = call(
        slot_sum_kernel, [((side, width), bf16)] * 3, (send, d_first, edge_first), flops=dense, name="slot_sum"
    )
    got_low = lax.ppermute(back_high, "lon", ring(lon_count, 1))
    got_high = lax.ppermute(back_low, "lon", ring(lon_count, -1))
    (mesh_parts,) = to_owners(d_first)
    (edge_grad,) = call(
        edge_grad_kernel, [((edges, width), bf16)], (d_first, edge_first), flops=dense, name="edge_grad"
    )
    (grid_grad,) = call(
        grid_grad_kernel,
        [((grid_rows, width), bf16)],
        (send_rows, got_low, back_own, got_high),
        flops=2 * listed * grid_rows * width,
        name="grid_grad",
    )
    (mesh_grad,) = call(
        mesh_grad_kernel, [((own, width), bf16)], (mesh_parts, direct, edge_first), name="mesh_grad"
    )
    return (mesh_out, grid_grad, mesh_grad, edge_grad)


def solution(mesh):
    fine = Mesh(mesh.devices.reshape(mesh.shape["lon"], 8, 4, 2), ("lon", "z", "y", "core"))
    every = ("lon", "z", "y", "core")
    rows = P(every, None)
    flat = P(every)
    patch = P("lon", None)
    return jax.shard_map(
        shards,
        mesh=fine,
        in_specs=(rows, patch, rows, patch, flat, flat, rows, flat) + (P(),) * 6,
        out_specs=(rows, rows, rows, rows),
        check_vma=False,
    )
```

```python
import jax
import jax.numpy as jnp
from jax import lax
from jax.experimental import pallas as pl
from jax.experimental.pallas import tpu as pltpu
from jax.sharding import Mesh
from jax.sharding import PartitionSpec as P

eps = 1e-05
f32 = jnp.float32
bf16 = jnp.bfloat16
i32 = jnp.int32

LANES = 128
CHUNK = 256
MIB = 1 << 20


def dot(a, b):
    return lax.dot_general(a, b, (((1,), (0,)), ((), ())), preferred_element_type=f32)


def dot_nt(a, b):
    return lax.dot_general(a, b, (((1,), (1,)), ((), ())), preferred_element_type=f32)


def dot_tn(a, b):
    return lax.dot_general(a, b, (((0,), (0,)), ((), ())), preferred_element_type=f32)


def split_dot_nt(a, b):
    high = a.astype(bf16)
    low = (a - high.astype(f32)).astype(bf16)
    return dot_nt(high, b) + dot_nt(low, b)


def one_hot(mask):
    return jnp.where(mask, 1.0, 0.0).astype(bf16)


def call(kernel, outs, args, smem=(), hbm=(), scratch=(), limit=16, flops=0, name=None):
    def space(i):
        if i in smem:
            return pltpu.SMEM
        return pltpu.HBM if i in hbm else pltpu.VMEM

    return pl.pallas_call(
        kernel,
        out_shape=[jax.ShapeDtypeStruct(s, d) for s, d in outs],
        in_specs=[pl.BlockSpec(memory_space=space(i)) for i in range(len(args))],
        out_specs=[pl.BlockSpec(memory_space=pltpu.VMEM) for _ in outs],
        scratch_shapes=list(scratch),
        compiler_params=pltpu.CompilerParams(vmem_limit_bytes=limit * MIB),
        cost_estimate=pl.CostEstimate(flops=flops, bytes_accessed=0, transcendentals=0),
        name=name,
    )(*args)


def column(cols, start, size):
    parts = [cols[:, j : j + 1] for j in range(start // LANES, (start + size) // LANES)]
    return parts[0] if len(parts) == 1 else jnp.concatenate(parts, axis=0)


def row_hot(spot, rows, start, size):
    parts = [one_hot(spot == rows[j : j + 1, :]) for j in range(start // LANES, (start + size) // LANES)]
    return jnp.concatenate(parts, axis=1)


def chunks(rows, size):
    return [(at, slice(at, at + size)) for at in range(0, rows, size)]


def live_rows(rows_ref, count):
    rows = rows_ref[...]
    slot = lax.broadcasted_iota(i32, rows.shape, 0) * LANES + lax.broadcasted_iota(
        i32, rows.shape, 1
    )
    return jnp.where(slot < count, rows, -1)


def row_index_kernel(out_ref):
    out_ref[...] = lax.broadcasted_iota(i32, out_ref.shape, 0)


def halo_rows_kernel(
    index_ref, list_ref, grid_ref, count_ref, recv_ref, low_ref, own_ref, high_ref, live_ref
):
    rows = dot_tn(one_hot(index_ref[...] == list_ref[...]), grid_ref[...]).astype(bf16)
    side = rows.shape[0] // 3
    low_ref[...] = rows[0:side]
    own_ref[...] = rows[side : 2 * side]
    high_ref[...] = rows[2 * side :]
    live_ref[...] = live_rows(recv_ref, count_ref[...])


def mesh_rows_kernel(live_ref, mesh_ref, gain_ref, out_ref, own_ref, gain_out_ref):
    gain_out_ref[...] = gain_ref[...]
    own = own_ref.shape[0]
    own_ref[...] = mesh_ref[pl.ds(pl.multiple_of(my_block() * own, own), own), :]
    m = mesh_ref.shape[0]
    cols = jnp.transpose(live_ref[...])
    for start, at in chunks(out_ref.shape[0], LANES):
        hot = one_hot(lax.broadcasted_iota(i32, (LANES, m), 1) == column(cols, start, LANES))
        out_ref[at, :] = dot(hot, mesh_ref[...]).astype(bf16)


def edge_forward_kernel(
    send_ref, edge_ref, mesh_rows_ref, low_ref, own_ref, high_ref, first_ref, second_ref,
    normed_ref, slope_ref, work_ref, post_ref,
):
    listed = jnp.concatenate([low_ref[...], own_ref[...], high_ref[...]], axis=0)
    n = listed.shape[0]
    cols = jnp.transpose(send_ref[...])
    parts = chunks(edge_ref.shape[0], CHUNK)
    for start, at in parts:
        hot = one_hot(lax.broadcasted_iota(i32, (CHUNK, n), 1) == column(cols, start, CHUNK))
        source = dot(hot, listed).astype(bf16)
        given = jnp.concatenate([edge_ref[at, :], source, mesh_rows_ref[at, :]], axis=1)
        work_ref[at, :] = dot(given, first_ref[...])
    for _, at in parts:
        first = work_ref[at, :]
        sigma = jax.nn.sigmoid(first)
        act = first * sigma
        work_ref[at, :] = sigma + act * (1.0 - sigma)
        post_ref[at, :] = dot(act.astype(bf16), second_ref[...])
    for _, at in parts:
        normed, factor = norm(post_ref[at, :])
        normed_ref[at, :] = normed.astype(bf16)
        slope_ref[at, :] = (factor * work_ref[at, :]).astype(bf16)


def my_core():
    return lax.axis_index("core").astype(i32)


def my_block():
    return (lax.axis_index("z") * 8 + lax.axis_index("y") * 2 + lax.axis_index("core")).astype(i32)


def my_lane(shift):
    return lax.rem(lax.axis_index("y").astype(i32) + shift, lax.axis_size("y"))


def block_sum(own, y, core, live, value_ref):
    lanes = lax.axis_size("y")
    i = lax.broadcasted_iota(i32, (own * lax.axis_size("z"), LANES), 0)
    spot = (i // own) * (2 * lanes * own) + (2 * y + core) * own + i % own
    total = jnp.zeros((spot.shape[0], value_ref.shape[1]), f32)
    for begin, at in chunks(value_ref.shape[0], CHUNK):
        total = total + dot(row_hot(spot, live, begin, CHUNK), value_ref[at, :])
    return total


SHIFTS = (2, 1, 3, 0)


def half_sum_kernel(own, here, live_ref, value_ref, out_ref):
    live = live_ref[...]
    core = my_core() if here else 1 - my_core()
    size = out_ref.shape[0] // len(SHIFTS)
    for n, shift in enumerate(SHIFTS):
        total = block_sum(own, my_lane(shift), core, live, value_ref)
        out_ref[n * size : (n + 1) * size, :] = total.astype(out_ref.dtype)


def half_first_kernel(
    own, live_ref, value_ref, cot_ref, node_gain_ref, edge_gain_ref, out_ref, own_cot_ref, gains_ref
):
    half_sum_kernel(own, True, live_ref, value_ref, out_ref)
    own_cot_ref[...] = cot_ref[pl.ds(pl.multiple_of(my_block() * own, own), own), :]
    gains_ref[0:1, :] = node_gain_ref[...]
    gains_ref[1:2, :] = edge_gain_ref[...]


def pieces_kernel(here_ref, away_ref, *out_refs):
    size = here_ref.shape[0] // len(out_refs)
    for n, out_ref in enumerate(out_refs):
        at = slice(n * size, (n + 1) * size)
        out_ref[...] = (here_ref[at, :] + away_ref[at, :].astype(f32)).astype(out_ref.dtype)


def total_kernel(a_ref, b_ref, c_ref, here_ref, out_ref):
    far = a_ref[...].astype(f32) + (b_ref[...].astype(f32) + c_ref[...].astype(f32))
    out_ref[...] = (here_ref[...] + far).astype(bf16).reshape(out_ref.shape)


def norm(value):
    center = value - jnp.mean(value, axis=-1, keepdims=True)
    factor = lax.rsqrt(jnp.mean(center * center, axis=-1, keepdims=True) + eps)
    return center * factor, factor


def node_kernel(
    parts_ref, mesh_ref, cot_ref, first_ref, second_ref, gains_ref, grad_ref, normed_ref, d_pre_ref,
):
    width = mesh_ref.shape[1]
    aggregate = jnp.sum(parts_ref[...].astype(f32), axis=0)
    agg_low = (aggregate * gains_ref[1:2, :]).astype(bf16)
    mesh = mesh_ref[...]
    gain = gains_ref[0:1, :]
    pre = dot(mesh, first_ref[0:width, :]) + dot(agg_low, first_ref[width : 2 * width, :])
    sigma = jax.nn.sigmoid(pre)
    act = (pre * sigma).astype(bf16)
    post = dot(act, second_ref[...])
    normed, factor = norm(post)
    normed_ref[...] = normed
    scaled = cot_ref[...].astype(f32) * gain
    d_post = factor * (
        scaled
        - jnp.mean(scaled, axis=-1, keepdims=True)
        - normed * jnp.mean(scaled * normed, axis=-1, keepdims=True)
    )
    d_pre = dot_nt(d_post.astype(bf16), second_ref[...]) * (sigma * (1.0 + pre * (1.0 - sigma)))
    d_pre = d_pre.astype(bf16)
    grad = dot_nt(d_pre, first_ref[width : 2 * width, :]).astype(bf16)
    grad_ref[...] = jnp.broadcast_to(grad[None], grad_ref.shape)
    d_pre_ref[...] = d_pre


def mesh_out_kernel(
    mesh_ref, cot_ref, normed_ref, d_pre_ref, first_ref, gains_ref, out_ref, direct_ref
):
    width = mesh_ref.shape[1]
    out_ref[...] = (mesh_ref[...].astype(f32) + normed_ref[...] * gains_ref[0:1, :]).astype(bf16)
    direct_ref[...] = cot_ref[...].astype(f32) + dot_nt(d_pre_ref[...], first_ref[0:width, :])


def half_place(own, core, live):
    place = (live // (2 * own)) * own + live % own
    return jnp.where((live // own) % 2 == core, place, -1)


def near_rows_kernel(own, live_ref, near_ref, out_ref):
    half = near_ref.shape[0]
    place = half_place(own, my_core(), live_ref[...])
    cols = jnp.transpose(place)
    for start, at in chunks(out_ref.shape[0], LANES):
        hot = one_hot(lax.broadcasted_iota(i32, (LANES, half), 1) == column(cols, start, LANES))
        out_ref[at, :] = dot(hot, near_ref[...]).astype(bf16)


def edge_backward_kernel(
    own, live_ref, near_rows_ref, far_ref, normed_ref, slope_ref, second_ref,
    gains_ref, out_ref, work_ref,
):
    half = far_ref.shape[0]
    place = half_place(own, 1 - my_core(), live_ref[...])
    cols = jnp.transpose(place)
    for start, at in chunks(out_ref.shape[0], LANES):
        hot = one_hot(lax.broadcasted_iota(i32, (LANES, half), 1) == column(cols, start, LANES))
        work_ref[at, :] = dot(hot, far_ref[...]) + near_rows_ref[at, :].astype(f32)
    gain = gains_ref[1:2, :]
    for _, at in chunks(out_ref.shape[0], CHUNK):
        scaled = work_ref[at, :] * gain
        normed = normed_ref[at, :].astype(f32)
        inner = (
            scaled
            - jnp.mean(scaled, axis=-1, keepdims=True)
            - normed * jnp.mean(scaled * normed, axis=-1, keepdims=True)
        ).astype(bf16)
        out_ref[at, :] = (dot_nt(inner, second_ref[...]) * slope_ref[at, :].astype(f32)).astype(bf16)


def slot_sum_kernel(send_ref, d_first_ref, first_ref, low_ref, own_ref, high_ref):
    width = d_first_ref.shape[1]
    side = low_ref.shape[0]
    spot = lax.broadcasted_iota(i32, (3 * side, LANES), 0)
    total = jnp.zeros((3 * side, width), f32)
    for start, at in chunks(d_first_ref.shape[0], CHUNK):
        total = total + dot(row_hot(spot, send_ref, start, CHUNK), d_first_ref[at, :])
    terms = split_dot_nt(total, first_ref[width : 2 * width, :]).astype(bf16)
    low_ref[...] = terms[0:side]
    own_ref[...] = terms[side : 2 * side]
    high_ref[...] = terms[2 * side :]


def edge_grad_kernel(d_first_ref, first_ref, out_ref):
    width = d_first_ref.shape[1]
    for i in range(out_ref.shape[0] // CHUNK):
        at = slice(i * CHUNK, (i + 1) * CHUNK)
        out_ref[at, :] = dot_nt(d_first_ref[at, :], first_ref[0:width, :]).astype(bf16)


def grid_grad_kernel(list_ref, low_ref, own_ref, high_ref, out_ref):
    terms = jnp.concatenate([low_ref[...], own_ref[...], high_ref[...]], axis=0)
    spot = lax.broadcasted_iota(i32, (out_ref.shape[0], terms.shape[0]), 0)
    out_ref[...] = dot(one_hot(spot == list_ref[...]), terms).astype(bf16)


def mesh_grad_kernel(parts_ref, direct_ref, first_ref, out_ref):
    width = direct_ref.shape[1]
    total = jnp.sum(parts_ref[...].astype(f32), axis=0)
    out_ref[...] = (
        direct_ref[...] + split_dot_nt(total, first_ref[2 * width : 3 * width, :])
    ).astype(bf16)


def ring(count, shift):
    return [(i, (i + shift) % count) for i in range(count)]


def shards(
    grid_latent,
    mesh_latent,
    edge_latent,
    mesh_cotangent,
    edge_senders,
    edge_receivers,
    send_rows,
    edge_count,
    edge_first,
    edge_second,
    edge_gain,
    node_first,
    node_second,
    node_gain,
):
    width = grid_latent.shape[1]
    zy = ("z", "y")
    lon_count = lax.axis_size("lon")
    owners = lax.axis_size("z") * lax.axis_size("y")
    listed = send_rows.shape[1]
    side = listed // 3
    patch = mesh_latent.shape[0]
    own = patch // (2 * owners)
    half = patch // 2
    edges = edge_latent.shape[0]
    grid_rows = grid_latent.shape[0]
    recv = edge_receivers.reshape(edges // LANES, LANES)
    send = edge_senders.reshape(edges // LANES, LANES)
    swap = [(0, 1), (1, 0)]
    big = 2 * edges * patch * width
    dense = 2 * edges * width * width

    vm = pltpu.VMEM
    (index,) = call(
        row_index_kernel, [((grid_rows, listed), i32)], (), flops=2 * big, name="row_index"
    )
    to_low, stay, to_high, live = call(
        halo_rows_kernel,
        [((side, width), bf16)] * 3 + [(recv.shape, i32)],
        (index, send_rows, grid_latent, edge_count.reshape(1, 1), recv),
        flops=2 * big,
        name="halo_rows",
    )
    from_low = lax.ppermute(to_high, "lon", ring(lon_count, 1))
    from_high = lax.ppermute(to_low, "lon", ring(lon_count, -1))
    mesh_rows, own_mesh, node_gain_row = call(
        mesh_rows_kernel,
        [((edges, width), bf16), ((own, width), bf16), ((1, width), f32)],
        (live, mesh_latent, node_gain.reshape(1, width)),
        flops=big,
        name="mesh_rows",
    )
    normed, slope = call(
        edge_forward_kernel,
        [((edges, width), bf16)] * 2,
        (send, edge_latent, mesh_rows, from_low, stay, from_high, edge_first, edge_second),
        scratch=[vm((edges, width), f32)] * 2,
        flops=5 * dense,
        name="edge_forward",
    )

    lanes = lax.axis_size("y")
    columns = lax.axis_size("z")
    piece = columns * own

    def to_owners(value, extras=(), extra_outs=(), beside=None):
        (out,) = call(
            lambda *refs: half_sum_kernel(own, False, *refs), [((half, width), bf16)],
            (live, value), flops=big // 2, name="half_away",
        )
        away = lax.ppermute(out, "core", swap)
        here = call(
            (lambda *refs: half_first_kernel(own, *refs))
            if extras
            else (lambda *refs: half_sum_kernel(own, True, *refs)),
            [((half, width), f32)] + list(extra_outs),
            (live, value) + tuple(extras), flops=big // 2, name="half_here",
        )
        sums = call(
            pieces_kernel,
            [((piece, width), bf16 if shift else f32) for shift in SHIFTS],
            (here[0], away), name="pieces",
        )
        got = [
            lax.ppermute(total, "y", ring(lanes, shift)) if shift else total
            for shift, total in zip(SHIFTS, sums)
        ]
        done = ()
        if beside is not None:
            got[-1], *done = lax.optimization_barrier((got[-1], *beside()))
        (both,) = call(total_kernel, [((columns, own, width), bf16)], got, name="total")
        parts = lax.all_to_all(both, "z", 0, 0, tiled=True)
        return (parts,) + tuple(here[1:]) + tuple(done)

    parts, own_cot, gains = to_owners(
        normed,
        (mesh_cotangent, node_gain_row, edge_gain.reshape(1, width)),
        (((own, width), bf16), ((2, width), f32)),
    )
    grad_copies, node_normed, d_pre = call(
        node_kernel,
        [((owners, own, width), bf16), ((own, width), f32), ((own, width), bf16)],
        (parts, own_mesh, own_cot, node_first, node_second, gains),
        flops=2 * own * width * width * 7,
        name="node",
    )
    near = lax.all_to_all(grad_copies, zy, 0, 0, tiled=True).reshape(half, width)
    far = lax.ppermute(near, "core", swap)
    (near_rows,) = call(
        lambda *refs: near_rows_kernel(own, *refs), [((edges, width), bf16)],
        (live, near), flops=big // 2, name="near_rows",
    )
    (d_first,) = call(
        lambda *refs: edge_backward_kernel(own, *refs),
        [((edges, width), bf16)],
        (
            live, near_rows, far, normed, slope, edge_second,
            gains,
        ),
        scratch=[vm((edges, width), f32)],
        flops=big // 2 + dense,
        name="edge_backward",
    )
    def other_work():
        slots = call(
            slot_sum_kernel, [((side, width), bf16)] * 3, (send, d_first, edge_first),
            flops=dense, name="slot_sum",
        )
        grads = call(
            edge_grad_kernel, [((edges, width), bf16)], (d_first, edge_first),
            flops=dense, name="edge_grad",
        )
        late_normed, late_d_pre, _ = lax.optimization_barrier((node_normed, d_pre, d_first))
        node_outs = call(
            mesh_out_kernel,
            [((own, width), bf16), ((own, width), f32)],
            (own_mesh, own_cot, late_normed, late_d_pre, node_first, gains),
            flops=2 * own * width * width, name="mesh_out",
        )
        return (*slots, *grads, *node_outs)

    mesh_parts, back_low, back_own, back_high, edge_grad, mesh_out, direct = to_owners(
        d_first, beside=other_work
    )
    got_low = lax.ppermute(back_high, "lon", ring(lon_count, 1))
    got_high = lax.ppermute(back_low, "lon", ring(lon_count, -1))
    (grid_grad,) = call(
        grid_grad_kernel,
        [((grid_rows, width), bf16)],
        (send_rows, got_low, back_own, got_high),
        flops=2 * listed * grid_rows * width,
        name="grid_grad",
    )
    (mesh_grad,) = call(
        mesh_grad_kernel, [((own, width), bf16)], (mesh_parts, direct, edge_first), name="mesh_grad"
    )
    return (mesh_out, grid_grad, mesh_grad, edge_grad)


def solution(mesh):
    fine = Mesh(mesh.devices.reshape(mesh.shape["lon"], 8, 4, 2), ("lon", "z", "y", "core"))
    every = ("lon", "z", "y", "core")
    rows = P(every, None)
    flat = P(every)
    patch = P("lon", None)
    return jax.shard_map(
        shards,
        mesh=fine,
        in_specs=(rows, patch, rows, patch, flat, flat, rows, flat) + (P(),) * 6,
        out_specs=(rows, rows, rows, rows),
        check_vma=False,
    )
```

```python
import jax
import jax.numpy as jnp
from jax import lax
from jax.experimental import pallas as pl
from jax.experimental.pallas import tpu as pltpu
from jax.sharding import Mesh
from jax.sharding import PartitionSpec as P

eps = 1e-05
f32 = jnp.float32
bf16 = jnp.bfloat16
i32 = jnp.int32

LANES = 128
CHUNK = 256
MIB = 1 << 20


def dot(a, b):
    return lax.dot_general(a, b, (((1,), (0,)), ((), ())), preferred_element_type=f32)


def dot_nt(a, b):
    return lax.dot_general(a, b, (((1,), (1,)), ((), ())), preferred_element_type=f32)


def dot_tn(a, b):
    return lax.dot_general(a, b, (((0,), (0,)), ((), ())), preferred_element_type=f32)


def split_dot_nt(a, b):
    high = a.astype(bf16)
    low = (a - high.astype(f32)).astype(bf16)
    return dot_nt(high, b) + dot_nt(low, b)


def one_hot(mask):
    return jnp.where(mask, 1.0, 0.0).astype(bf16)


def call(kernel, outs, args, smem=(), hbm=(), scratch=(), limit=16, flops=0, name=None):
    def space(i):
        if i in smem:
            return pltpu.SMEM
        return pltpu.HBM if i in hbm else pltpu.VMEM

    return pl.pallas_call(
        kernel,
        out_shape=[jax.ShapeDtypeStruct(s, d) for s, d in outs],
        in_specs=[pl.BlockSpec(memory_space=space(i)) for i in range(len(args))],
        out_specs=[pl.BlockSpec(memory_space=pltpu.VMEM) for _ in outs],
        scratch_shapes=list(scratch),
        compiler_params=pltpu.CompilerParams(vmem_limit_bytes=limit * MIB),
        cost_estimate=pl.CostEstimate(flops=flops, bytes_accessed=0, transcendentals=0),
        name=name,
    )(*args)


def column(cols, start, size):
    parts = [cols[:, j : j + 1] for j in range(start // LANES, (start + size) // LANES)]
    return parts[0] if len(parts) == 1 else jnp.concatenate(parts, axis=0)


def row_hot(spot, rows, start, size):
    parts = [one_hot(spot == rows[j : j + 1, :]) for j in range(start // LANES, (start + size) // LANES)]
    return jnp.concatenate(parts, axis=1)


def chunks(rows, size):
    return [(at, slice(at, at + size)) for at in range(0, rows, size)]


def live_rows(rows_ref, count):
    rows = rows_ref[...]
    slot = lax.broadcasted_iota(i32, rows.shape, 0) * LANES + lax.broadcasted_iota(
        i32, rows.shape, 1
    )
    return jnp.where(slot < count, rows, -1)


def row_index_kernel(out_ref):
    out_ref[...] = lax.broadcasted_iota(i32, out_ref.shape, 0)


def halo_rows_kernel(
    index_ref, list_ref, grid_ref, count_ref, recv_ref, node_gain_ref, edge_gain_ref,
    low_ref, own_ref, high_ref, live_ref, gains_ref,
):
    gains_ref[0:1, :] = node_gain_ref[...]
    gains_ref[1:2, :] = edge_gain_ref[...]
    rows = dot_tn(one_hot(index_ref[...] == list_ref[...]), grid_ref[...]).astype(bf16)
    side = rows.shape[0] // 3
    low_ref[...] = rows[0:side]
    own_ref[...] = rows[side : 2 * side]
    high_ref[...] = rows[2 * side :]
    live_ref[...] = live_rows(recv_ref, count_ref[...])


def mesh_rows_kernel(live_ref, mesh_ref, out_ref, own_ref):
    own = own_ref.shape[0]
    own_ref[...] = mesh_ref[pl.ds(pl.multiple_of(my_block() * own, own), own), :]
    m = mesh_ref.shape[0]
    cols = jnp.transpose(live_ref[...])
    for start, at in chunks(out_ref.shape[0], LANES):
        hot = one_hot(lax.broadcasted_iota(i32, (LANES, m), 1) == column(cols, start, LANES))
        out_ref[at, :] = dot(hot, mesh_ref[...]).astype(bf16)


def edge_forward_kernel(
    send_ref, edge_ref, mesh_rows_ref, low_ref, own_ref, high_ref, first_ref, second_ref,
    normed_ref, slope_ref, work_ref, post_ref,
):
    listed = jnp.concatenate([low_ref[...], own_ref[...], high_ref[...]], axis=0)
    n = listed.shape[0]
    cols = jnp.transpose(send_ref[...])
    parts = chunks(edge_ref.shape[0], CHUNK)
    for start, at in parts:
        hot = one_hot(lax.broadcasted_iota(i32, (CHUNK, n), 1) == column(cols, start, CHUNK))
        source = dot(hot, listed).astype(bf16)
        given = jnp.concatenate([edge_ref[at, :], source, mesh_rows_ref[at, :]], axis=1)
        work_ref[at, :] = dot(given, first_ref[...])
    for _, at in parts:
        first = work_ref[at, :]
        sigma = jax.nn.sigmoid(first)
        act = first * sigma
        work_ref[at, :] = sigma + act * (1.0 - sigma)
        post_ref[at, :] = dot(act.astype(bf16), second_ref[...])
    for _, at in parts:
        normed, factor = norm(post_ref[at, :])
        normed_ref[at, :] = normed.astype(bf16)
        slope_ref[at, :] = (factor * work_ref[at, :]).astype(bf16)


def my_core():
    return lax.axis_index("core").astype(i32)


def my_block():
    return (lax.axis_index("z") * 8 + lax.axis_index("y") * 2 + lax.axis_index("core")).astype(i32)


def my_lane(shift):
    return lax.rem(lax.axis_index("y").astype(i32) + shift, lax.axis_size("y"))


def block_sum(own, y, core, live, value_ref):
    lanes = lax.axis_size("y")
    i = lax.broadcasted_iota(i32, (own * lax.axis_size("z"), LANES), 0)
    spot = (i // own) * (2 * lanes * own) + (2 * y + core) * own + i % own
    total = jnp.zeros((spot.shape[0], value_ref.shape[1]), f32)
    for begin, at in chunks(value_ref.shape[0], CHUNK):
        total = total + dot(row_hot(spot, live, begin, CHUNK), value_ref[at, :])
    return total


SHIFTS = (1, 3, 2, 0)


def half_sum_kernel(own, here, live_ref, value_ref, out_ref):
    live = live_ref[...]
    core = my_core() if here else 1 - my_core()
    size = out_ref.shape[0] // len(SHIFTS)
    for n, shift in enumerate(SHIFTS):
        total = block_sum(own, my_lane(shift), core, live, value_ref)
        out_ref[n * size : (n + 1) * size, :] = total.astype(out_ref.dtype)


def half_first_kernel(own, live_ref, value_ref, cot_ref, out_ref, own_cot_ref):
    half_sum_kernel(own, True, live_ref, value_ref, out_ref)
    own_cot_ref[...] = cot_ref[pl.ds(pl.multiple_of(my_block() * own, own), own), :]


def pieces_kernel(here_ref, away_ref, *out_refs):
    size = here_ref.shape[0] // len(out_refs)
    for n, out_ref in enumerate(out_refs):
        at = slice(n * size, (n + 1) * size)
        out_ref[...] = (here_ref[at, :] + away_ref[at, :].astype(f32)).astype(out_ref.dtype)


def total_kernel(a_ref, b_ref, c_ref, here_ref, out_ref):
    far = a_ref[...].astype(f32) + (b_ref[...].astype(f32) + c_ref[...].astype(f32))
    out_ref[...] = (here_ref[...] + far).astype(bf16).reshape(out_ref.shape)


def norm(value):
    center = value - jnp.mean(value, axis=-1, keepdims=True)
    factor = lax.rsqrt(jnp.mean(center * center, axis=-1, keepdims=True) + eps)
    return center * factor, factor


def node_kernel(
    parts_ref, mesh_ref, cot_ref, first_ref, second_ref, gains_ref, grad_ref, normed_ref, d_pre_ref,
):
    width = mesh_ref.shape[1]
    aggregate = jnp.sum(parts_ref[...].astype(f32), axis=0)
    agg_low = (aggregate * gains_ref[1:2, :]).astype(bf16)
    mesh = mesh_ref[...]
    gain = gains_ref[0:1, :]
    pre = dot(mesh, first_ref[0:width, :]) + dot(agg_low, first_ref[width : 2 * width, :])
    sigma = jax.nn.sigmoid(pre)
    act = (pre * sigma).astype(bf16)
    post = dot(act, second_ref[...])
    normed, factor = norm(post)
    normed_ref[...] = normed
    scaled = cot_ref[...].astype(f32) * gain
    d_post = factor * (
        scaled
        - jnp.mean(scaled, axis=-1, keepdims=True)
        - normed * jnp.mean(scaled * normed, axis=-1, keepdims=True)
    )
    d_pre = dot_nt(d_post.astype(bf16), second_ref[...]) * (sigma * (1.0 + pre * (1.0 - sigma)))
    d_pre = d_pre.astype(bf16)
    grad = dot_nt(d_pre, first_ref[width : 2 * width, :]).astype(bf16)
    grad_ref[...] = jnp.broadcast_to(grad[None], grad_ref.shape)
    d_pre_ref[...] = d_pre


def mesh_out_kernel(
    mesh_ref, cot_ref, normed_ref, d_pre_ref, first_ref, gains_ref, out_ref, direct_ref
):
    width = mesh_ref.shape[1]
    out_ref[...] = (mesh_ref[...].astype(f32) + normed_ref[...] * gains_ref[0:1, :]).astype(bf16)
    direct_ref[...] = cot_ref[...].astype(f32) + dot_nt(d_pre_ref[...], first_ref[0:width, :])


def half_place(own, core, live):
    place = (live // (2 * own)) * own + live % own
    return jnp.where((live // own) % 2 == core, place, -1)


def near_rows_kernel(own, live_ref, near_ref, out_ref):
    half = near_ref.shape[0]
    place = half_place(own, my_core(), live_ref[...])
    cols = jnp.transpose(place)
    for start, at in chunks(out_ref.shape[0], LANES):
        hot = one_hot(lax.broadcasted_iota(i32, (LANES, half), 1) == column(cols, start, LANES))
        out_ref[at, :] = dot(hot, near_ref[...]).astype(bf16)


def edge_backward_kernel(
    own, live_ref, near_rows_ref, far_ref, normed_ref, slope_ref, second_ref,
    gains_ref, out_ref, work_ref,
):
    half = far_ref.shape[0]
    place = half_place(own, 1 - my_core(), live_ref[...])
    cols = jnp.transpose(place)
    for start, at in chunks(out_ref.shape[0], LANES):
        hot = one_hot(lax.broadcasted_iota(i32, (LANES, half), 1) == column(cols, start, LANES))
        work_ref[at, :] = dot(hot, far_ref[...]) + near_rows_ref[at, :].astype(f32)
    gain = gains_ref[1:2, :]
    for _, at in chunks(out_ref.shape[0], CHUNK):
        scaled = work_ref[at, :] * gain
        normed = normed_ref[at, :].astype(f32)
        inner = (
            scaled
            - jnp.mean(scaled, axis=-1, keepdims=True)
            - normed * jnp.mean(scaled * normed, axis=-1, keepdims=True)
        ).astype(bf16)
        out_ref[at, :] = (dot_nt(inner, second_ref[...]) * slope_ref[at, :].astype(f32)).astype(bf16)


def slot_sum_kernel(send_ref, d_first_ref, first_ref, low_ref, own_ref, high_ref):
    width = d_first_ref.shape[1]
    side = low_ref.shape[0]
    spot = lax.broadcasted_iota(i32, (3 * side, LANES), 0)
    total = jnp.zeros((3 * side, width), f32)
    for start, at in chunks(d_first_ref.shape[0], CHUNK):
        total = total + dot(row_hot(spot, send_ref, start, CHUNK), d_first_ref[at, :])
    terms = split_dot_nt(total, first_ref[width : 2 * width, :]).astype(bf16)
    low_ref[...] = terms[0:side]
    own_ref[...] = terms[side : 2 * side]
    high_ref[...] = terms[2 * side :]


def edge_grad_kernel(d_first_ref, first_ref, out_ref):
    width = d_first_ref.shape[1]
    for i in range(out_ref.shape[0] // CHUNK):
        at = slice(i * CHUNK, (i + 1) * CHUNK)
        out_ref[at, :] = dot_nt(d_first_ref[at, :], first_ref[0:width, :]).astype(bf16)


def grid_grad_kernel(list_ref, low_ref, own_ref, high_ref, out_ref):
    terms = jnp.concatenate([low_ref[...], own_ref[...], high_ref[...]], axis=0)
    spot = lax.broadcasted_iota(i32, (out_ref.shape[0], terms.shape[0]), 0)
    out_ref[...] = dot(one_hot(spot == list_ref[...]), terms).astype(bf16)


def mesh_grad_kernel(parts_ref, direct_ref, first_ref, out_ref):
    width = direct_ref.shape[1]
    total = jnp.sum(parts_ref[...].astype(f32), axis=0)
    out_ref[...] = (
        direct_ref[...] + split_dot_nt(total, first_ref[2 * width : 3 * width, :])
    ).astype(bf16)


def ring(count, shift):
    return [(i, (i + shift) % count) for i in range(count)]


def shards(
    grid_latent,
    mesh_latent,
    edge_latent,
    mesh_cotangent,
    edge_senders,
    edge_receivers,
    send_rows,
    edge_count,
    edge_first,
    edge_second,
    edge_gain,
    node_first,
    node_second,
    node_gain,
):
    width = grid_latent.shape[1]
    zy = ("z", "y")
    lon_count = lax.axis_size("lon")
    owners = lax.axis_size("z") * lax.axis_size("y")
    listed = send_rows.shape[1]
    side = listed // 3
    patch = mesh_latent.shape[0]
    own = patch // (2 * owners)
    half = patch // 2
    edges = edge_latent.shape[0]
    grid_rows = grid_latent.shape[0]
    recv = edge_receivers.reshape(edges // LANES, LANES)
    send = edge_senders.reshape(edges // LANES, LANES)
    swap = [(0, 1), (1, 0)]
    big = 2 * edges * patch * width
    dense = 2 * edges * width * width

    vm = pltpu.VMEM
    (index,) = call(
        row_index_kernel, [((grid_rows, listed), i32)], (), flops=2 * big, name="row_index"
    )
    to_low, stay, to_high, live, gains = call(
        halo_rows_kernel,
        [((side, width), bf16)] * 3 + [(recv.shape, i32), ((2, width), f32)],
        (
            index, send_rows, grid_latent, edge_count.reshape(1, 1), recv,
            node_gain.reshape(1, width), edge_gain.reshape(1, width),
        ),
        flops=2 * big,
        name="halo_rows",
    )
    from_low = lax.ppermute(to_high, "lon", ring(lon_count, 1))
    from_high = lax.ppermute(to_low, "lon", ring(lon_count, -1))
    mesh_rows, own_mesh = call(
        mesh_rows_kernel,
        [((edges, width), bf16), ((own, width), bf16)],
        (live, mesh_latent),
        flops=big,
        name="mesh_rows",
    )
    normed, slope = call(
        edge_forward_kernel,
        [((edges, width), bf16)] * 2,
        (send, edge_latent, mesh_rows, from_low, stay, from_high, edge_first, edge_second),
        scratch=[vm((edges, width), f32)] * 2,
        flops=5 * dense,
        name="edge_forward",
    )

    lanes = lax.axis_size("y")
    columns = lax.axis_size("z")
    piece = columns * own

    def to_owners(value, extras=(), extra_outs=(), beside=None):
        (out,) = call(
            lambda *refs: half_sum_kernel(own, False, *refs), [((half, width), bf16)],
            (live, value), flops=big // 2, name="half_away",
        )
        away = lax.ppermute(out, "core", swap)
        here = call(
            (lambda *refs: half_first_kernel(own, *refs))
            if extras
            else (lambda *refs: half_sum_kernel(own, True, *refs)),
            [((half, width), f32)] + list(extra_outs),
            (live, value) + tuple(extras), flops=big // 2, name="half_here",
        )
        sums = call(
            pieces_kernel,
            [((piece, width), bf16 if shift else f32) for shift in SHIFTS],
            (here[0], away), name="pieces",
        )
        got = [
            lax.ppermute(total, "y", ring(lanes, shift)) if shift else total
            for shift, total in zip(SHIFTS, sums)
        ]
        done = ()
        if beside is not None:
            got[-1], *done = lax.optimization_barrier((got[-1], *beside()))
        (both,) = call(total_kernel, [((columns, own, width), bf16)], got, name="total")
        parts = lax.all_to_all(both, "z", 0, 0, tiled=True)
        return (parts,) + tuple(here[1:]) + tuple(done)

    parts, own_cot = to_owners(normed, (mesh_cotangent,), (((own, width), bf16),))
    grad_copies, node_normed, d_pre = call(
        node_kernel,
        [((owners, own, width), bf16), ((own, width), f32), ((own, width), bf16)],
        (parts, own_mesh, own_cot, node_first, node_second, gains),
        flops=2 * own * width * width * 7,
        name="node",
    )
    near = lax.all_to_all(grad_copies, zy, 0, 0, tiled=True).reshape(half, width)
    far = lax.ppermute(near, "core", swap)
    (near_rows,) = call(
        lambda *refs: near_rows_kernel(own, *refs), [((edges, width), bf16)],
        (live, near), flops=big // 2, name="near_rows",
    )
    (d_first,) = call(
        lambda *refs: edge_backward_kernel(own, *refs),
        [((edges, width), bf16)],
        (
            live, near_rows, far, normed, slope, edge_second,
            gains,
        ),
        scratch=[vm((edges, width), f32)],
        flops=big // 2 + dense,
        name="edge_backward",
    )
    def other_work():
        slots = call(
            slot_sum_kernel, [((side, width), bf16)] * 3, (send, d_first, edge_first),
            flops=dense, name="slot_sum",
        )
        grads = call(
            edge_grad_kernel, [((edges, width), bf16)], (d_first, edge_first),
            flops=dense, name="edge_grad",
        )
        late_normed, late_d_pre, _ = lax.optimization_barrier((node_normed, d_pre, d_first))
        node_outs = call(
            mesh_out_kernel,
            [((own, width), bf16), ((own, width), f32)],
            (own_mesh, own_cot, late_normed, late_d_pre, node_first, gains),
            flops=2 * own * width * width, name="mesh_out",
        )
        return (*slots, *grads, *node_outs)

    mesh_parts, back_low, back_own, back_high, edge_grad, mesh_out, direct = to_owners(
        d_first, beside=other_work
    )
    got_low = lax.ppermute(back_high, "lon", ring(lon_count, 1))
    got_high = lax.ppermute(back_low, "lon", ring(lon_count, -1))
    (grid_grad,) = call(
        grid_grad_kernel,
        [((grid_rows, width), bf16)],
        (send_rows, got_low, back_own, got_high),
        flops=2 * listed * grid_rows * width,
        name="grid_grad",
    )
    (mesh_grad,) = call(
        mesh_grad_kernel, [((own, width), bf16)], (mesh_parts, direct, edge_first), name="mesh_grad"
    )
    return (mesh_out, grid_grad, mesh_grad, edge_grad)


def solution(mesh):
    fine = Mesh(mesh.devices.reshape(mesh.shape["lon"], 8, 4, 2), ("lon", "z", "y", "core"))
    every = ("lon", "z", "y", "core")
    rows = P(every, None)
    flat = P(every)
    patch = P("lon", None)
    return jax.shard_map(
        shards,
        mesh=fine,
        in_specs=(rows, patch, rows, patch, flat, flat, rows, flat) + (P(),) * 6,
        out_specs=(rows, rows, rows, rows),
        check_vma=False,
    )
```

```python
import jax
import jax.numpy as jnp
from jax import lax
from jax.experimental import pallas as pl
from jax.experimental.pallas import tpu as pltpu
from jax.sharding import Mesh
from jax.sharding import PartitionSpec as P

eps = 1e-05
f32 = jnp.float32
bf16 = jnp.bfloat16
i32 = jnp.int32

LANES = 128
CHUNK = 256
MIB = 1 << 20


def dot(a, b):
    return lax.dot_general(a, b, (((1,), (0,)), ((), ())), preferred_element_type=f32)


def dot_nt(a, b):
    return lax.dot_general(a, b, (((1,), (1,)), ((), ())), preferred_element_type=f32)


def dot_tn(a, b):
    return lax.dot_general(a, b, (((0,), (0,)), ((), ())), preferred_element_type=f32)


def split_dot_nt(a, b):
    high = a.astype(bf16)
    low = (a - high.astype(f32)).astype(bf16)
    return dot_nt(high, b) + dot_nt(low, b)


def one_hot(mask):
    return jnp.where(mask, 1.0, 0.0).astype(bf16)


def call(kernel, outs, args, smem=(), hbm=(), scratch=(), limit=16, flops=0, name=None):
    def space(i):
        if i in smem:
            return pltpu.SMEM
        return pltpu.HBM if i in hbm else pltpu.VMEM

    return pl.pallas_call(
        kernel,
        out_shape=[jax.ShapeDtypeStruct(s, d) for s, d in outs],
        in_specs=[pl.BlockSpec(memory_space=space(i)) for i in range(len(args))],
        out_specs=[pl.BlockSpec(memory_space=pltpu.VMEM) for _ in outs],
        scratch_shapes=list(scratch),
        compiler_params=pltpu.CompilerParams(vmem_limit_bytes=limit * MIB),
        cost_estimate=pl.CostEstimate(flops=flops, bytes_accessed=0, transcendentals=0),
        name=name,
    )(*args)


def column(cols, start, size):
    parts = [cols[:, j : j + 1] for j in range(start // LANES, (start + size) // LANES)]
    return parts[0] if len(parts) == 1 else jnp.concatenate(parts, axis=0)


def row_hot(spot, rows, start, size):
    parts = [one_hot(spot == rows[j : j + 1, :]) for j in range(start // LANES, (start + size) // LANES)]
    return jnp.concatenate(parts, axis=1)


def chunks(rows, size):
    return [(at, slice(at, at + size)) for at in range(0, rows, size)]


def live_rows(rows_ref, count):
    rows = rows_ref[...]
    slot = lax.broadcasted_iota(i32, rows.shape, 0) * LANES + lax.broadcasted_iota(
        i32, rows.shape, 1
    )
    return jnp.where(slot < count, rows, -1)


def row_index_kernel(out_ref):
    out_ref[...] = lax.broadcasted_iota(i32, out_ref.shape, 0)


def halo_rows_kernel(
    index_ref, list_ref, grid_ref, count_ref, recv_ref, node_gain_ref, edge_gain_ref,
    low_ref, own_ref, high_ref, live_ref, gains_ref,
):
    gains_ref[0:1, :] = node_gain_ref[...]
    gains_ref[1:2, :] = edge_gain_ref[...]
    rows = dot_tn(one_hot(index_ref[...] == list_ref[...]), grid_ref[...]).astype(bf16)
    side = rows.shape[0] // 3
    low_ref[...] = rows[0:side]
    own_ref[...] = rows[side : 2 * side]
    high_ref[...] = rows[2 * side :]
    live_ref[...] = live_rows(recv_ref, count_ref[...])


def mesh_rows_kernel(live_ref, mesh_ref, out_ref, own_ref):
    own = own_ref.shape[0]
    own_ref[...] = mesh_ref[pl.ds(pl.multiple_of(my_block() * own, own), own), :]
    m = mesh_ref.shape[0]
    cols = jnp.transpose(live_ref[...])
    for start, at in chunks(out_ref.shape[0], LANES):
        hot = one_hot(lax.broadcasted_iota(i32, (LANES, m), 1) == column(cols, start, LANES))
        out_ref[at, :] = dot(hot, mesh_ref[...]).astype(bf16)


def edge_forward_kernel(
    send_ref, edge_ref, mesh_rows_ref, low_ref, own_ref, high_ref, first_ref, second_ref,
    normed_ref, slope_ref, work_ref, post_ref,
):
    listed = jnp.concatenate([low_ref[...], own_ref[...], high_ref[...]], axis=0)
    n = listed.shape[0]
    cols = jnp.transpose(send_ref[...])
    parts = chunks(edge_ref.shape[0], CHUNK)
    for start, at in parts:
        hot = one_hot(lax.broadcasted_iota(i32, (CHUNK, n), 1) == column(cols, start, CHUNK))
        source = dot(hot, listed).astype(bf16)
        given = jnp.concatenate([edge_ref[at, :], source, mesh_rows_ref[at, :]], axis=1)
        work_ref[at, :] = dot(given, first_ref[...])
    for _, at in parts:
        first = work_ref[at, :]
        sigma = jax.nn.sigmoid(first)
        act = first * sigma
        work_ref[at, :] = sigma + act * (1.0 - sigma)
        post_ref[at, :] = dot(act.astype(bf16), second_ref[...])
    for _, at in parts:
        normed, factor = norm(post_ref[at, :])
        normed_ref[at, :] = normed.astype(bf16)
        slope_ref[at, :] = (factor * work_ref[at, :]).astype(bf16)


def my_core():
    return lax.axis_index("core").astype(i32)


def my_block():
    return (lax.axis_index("z") * 8 + lax.axis_index("y") * 2 + lax.axis_index("core")).astype(i32)


def my_lane(shift):
    return lax.rem(lax.axis_index("y").astype(i32) + shift, lax.axis_size("y"))


def block_sum(own, y, core, live, value_ref):
    lanes = lax.axis_size("y")
    i = lax.broadcasted_iota(i32, (own * lax.axis_size("z"), LANES), 0)
    spot = (i // own) * (2 * lanes * own) + (2 * y + core) * own + i % own
    total = jnp.zeros((spot.shape[0], value_ref.shape[1]), f32)
    for begin, at in chunks(value_ref.shape[0], CHUNK):
        total = total + dot(row_hot(spot, live, begin, CHUNK), value_ref[at, :])
    return total


SHIFTS = (1, 3, 2, 0)


def half_sum_kernel(own, here, live_ref, value_ref, out_ref):
    live = live_ref[...]
    core = my_core() if here else 1 - my_core()
    size = out_ref.shape[0] // len(SHIFTS)
    for n, shift in enumerate(SHIFTS):
        total = block_sum(own, my_lane(shift), core, live, value_ref)
        out_ref[n * size : (n + 1) * size, :] = total.astype(out_ref.dtype)


def half_first_kernel(own, live_ref, value_ref, cot_ref, out_ref, own_cot_ref):
    half_sum_kernel(own, True, live_ref, value_ref, out_ref)
    own_cot_ref[...] = cot_ref[pl.ds(pl.multiple_of(my_block() * own, own), own), :]


def pieces_kernel(here_ref, away_ref, *out_refs):
    size = here_ref.shape[0] // len(out_refs)
    for n, out_ref in enumerate(out_refs):
        at = slice(n * size, (n + 1) * size)
        out_ref[...] = (here_ref[at, :] + away_ref[at, :].astype(f32)).astype(out_ref.dtype)


def total_kernel(a_ref, b_ref, c_ref, here_ref, out_ref):
    far = a_ref[...].astype(f32) + (b_ref[...].astype(f32) + c_ref[...].astype(f32))
    out_ref[...] = (here_ref[...] + far).astype(bf16).reshape(out_ref.shape)


def norm(value):
    center = value - jnp.mean(value, axis=-1, keepdims=True)
    factor = lax.rsqrt(jnp.mean(center * center, axis=-1, keepdims=True) + eps)
    return center * factor, factor


def node_kernel(
    parts_ref, mesh_ref, cot_ref, first_ref, second_ref, gains_ref, grad_ref, normed_ref, d_pre_ref,
):
    width = mesh_ref.shape[1]
    aggregate = jnp.sum(parts_ref[...].astype(f32), axis=0)
    agg_low = (aggregate * gains_ref[1:2, :]).astype(bf16)
    mesh = mesh_ref[...]
    gain = gains_ref[0:1, :]
    pre = dot(mesh, first_ref[0:width, :]) + dot(agg_low, first_ref[width : 2 * width, :])
    sigma = jax.nn.sigmoid(pre)
    act = (pre * sigma).astype(bf16)
    post = dot(act, second_ref[...])
    normed, factor = norm(post)
    normed_ref[...] = normed
    scaled = cot_ref[...].astype(f32) * gain
    d_post = factor * (
        scaled
        - jnp.mean(scaled, axis=-1, keepdims=True)
        - normed * jnp.mean(scaled * normed, axis=-1, keepdims=True)
    )
    d_pre = dot_nt(d_post.astype(bf16), second_ref[...]) * (sigma * (1.0 + pre * (1.0 - sigma)))
    d_pre = d_pre.astype(bf16)
    grad = dot_nt(d_pre, first_ref[width : 2 * width, :]).astype(bf16)
    gained = grad.astype(f32) * gains_ref[1:2, :]
    centered = (gained - jnp.mean(gained, axis=-1, keepdims=True)).astype(bf16)
    grad_ref[...] = jnp.broadcast_to(centered[None], grad_ref.shape)
    d_pre_ref[...] = d_pre


def mesh_out_kernel(
    mesh_ref, cot_ref, normed_ref, d_pre_ref, first_ref, gains_ref, out_ref, direct_ref
):
    width = mesh_ref.shape[1]
    out_ref[...] = (mesh_ref[...].astype(f32) + normed_ref[...] * gains_ref[0:1, :]).astype(bf16)
    direct_ref[...] = cot_ref[...].astype(f32) + dot_nt(d_pre_ref[...], first_ref[0:width, :])


def half_place(own, core, live):
    place = (live // (2 * own)) * own + live % own
    return jnp.where((live // own) % 2 == core, place, -1)


def near_rows_kernel(own, live_ref, near_ref, out_ref):
    half = near_ref.shape[0]
    place = half_place(own, my_core(), live_ref[...])
    cols = jnp.transpose(place)
    for start, at in chunks(out_ref.shape[0], LANES):
        hot = one_hot(lax.broadcasted_iota(i32, (LANES, half), 1) == column(cols, start, LANES))
        out_ref[at, :] = dot(hot, near_ref[...]).astype(bf16)


def edge_backward_kernel(
    own, live_ref, near_rows_ref, far_ref, normed_ref, slope_ref, second_ref,
    out_ref, work_ref,
):
    half = far_ref.shape[0]
    place = half_place(own, 1 - my_core(), live_ref[...])
    cols = jnp.transpose(place)
    for start, at in chunks(out_ref.shape[0], LANES):
        hot = one_hot(lax.broadcasted_iota(i32, (LANES, half), 1) == column(cols, start, LANES))
        work_ref[at, :] = dot(hot, far_ref[...]) + near_rows_ref[at, :].astype(f32)
    for _, at in chunks(out_ref.shape[0], CHUNK):
        centered = work_ref[at, :]
        normed = normed_ref[at, :].astype(f32)
        inner = centered - normed * jnp.mean(centered * normed, axis=-1, keepdims=True)
        inner = inner.astype(bf16)
        out_ref[at, :] = (dot_nt(inner, second_ref[...]) * slope_ref[at, :].astype(f32)).astype(bf16)


def slot_sum_kernel(send_ref, d_first_ref, first_ref, low_ref, own_ref, high_ref):
    width = d_first_ref.shape[1]
    side = low_ref.shape[0]
    spot = lax.broadcasted_iota(i32, (3 * side, LANES), 0)
    total = jnp.zeros((3 * side, width), f32)
    for start, at in chunks(d_first_ref.shape[0], CHUNK):
        total = total + dot(row_hot(spot, send_ref, start, CHUNK), d_first_ref[at, :])
    terms = split_dot_nt(total, first_ref[width : 2 * width, :]).astype(bf16)
    low_ref[...] = terms[0:side]
    own_ref[...] = terms[side : 2 * side]
    high_ref[...] = terms[2 * side :]


def edge_grad_kernel(d_first_ref, first_ref, out_ref):
    width = d_first_ref.shape[1]
    for i in range(out_ref.shape[0] // CHUNK):
        at = slice(i * CHUNK, (i + 1) * CHUNK)
        out_ref[at, :] = dot_nt(d_first_ref[at, :], first_ref[0:width, :]).astype(bf16)


def grid_grad_kernel(list_ref, low_ref, own_ref, high_ref, out_ref):
    terms = jnp.concatenate([low_ref[...], own_ref[...], high_ref[...]], axis=0)
    spot = lax.broadcasted_iota(i32, (out_ref.shape[0], terms.shape[0]), 0)
    out_ref[...] = dot(one_hot(spot == list_ref[...]), terms).astype(bf16)


def mesh_grad_kernel(parts_ref, direct_ref, first_ref, out_ref):
    width = direct_ref.shape[1]
    total = jnp.sum(parts_ref[...].astype(f32), axis=0)
    out_ref[...] = (
        direct_ref[...] + split_dot_nt(total, first_ref[2 * width : 3 * width, :])
    ).astype(bf16)


def ring(count, shift):
    return [(i, (i + shift) % count) for i in range(count)]


def shards(
    grid_latent,
    mesh_latent,
    edge_latent,
    mesh_cotangent,
    edge_senders,
    edge_receivers,
    send_rows,
    edge_count,
    edge_first,
    edge_second,
    edge_gain,
    node_first,
    node_second,
    node_gain,
):
    width = grid_latent.shape[1]
    zy = ("z", "y")
    lon_count = lax.axis_size("lon")
    owners = lax.axis_size("z") * lax.axis_size("y")
    listed = send_rows.shape[1]
    side = listed // 3
    patch = mesh_latent.shape[0]
    own = patch // (2 * owners)
    half = patch // 2
    edges = edge_latent.shape[0]
    grid_rows = grid_latent.shape[0]
    recv = edge_receivers.reshape(edges // LANES, LANES)
    send = edge_senders.reshape(edges // LANES, LANES)
    swap = [(0, 1), (1, 0)]
    big = 2 * edges * patch * width
    dense = 2 * edges * width * width

    vm = pltpu.VMEM
    (index,) = call(
        row_index_kernel, [((grid_rows, listed), i32)], (), flops=2 * big, name="row_index"
    )
    to_low, stay, to_high, live, gains = call(
        halo_rows_kernel,
        [((side, width), bf16)] * 3 + [(recv.shape, i32), ((2, width), f32)],
        (
            index, send_rows, grid_latent, edge_count.reshape(1, 1), recv,
            node_gain.reshape(1, width), edge_gain.reshape(1, width),
        ),
        flops=2 * big,
        name="halo_rows",
    )
    from_low = lax.ppermute(to_high, "lon", ring(lon_count, 1))
    from_high = lax.ppermute(to_low, "lon", ring(lon_count, -1))
    mesh_rows, own_mesh = call(
        mesh_rows_kernel,
        [((edges, width), bf16), ((own, width), bf16)],
        (live, mesh_latent),
        flops=big,
        name="mesh_rows",
    )
    normed, slope = call(
        edge_forward_kernel,
        [((edges, width), bf16)] * 2,
        (send, edge_latent, mesh_rows, from_low, stay, from_high, edge_first, edge_second),
        scratch=[vm((edges, width), f32)] * 2,
        flops=5 * dense,
        name="edge_forward",
    )

    lanes = lax.axis_size("y")
    columns = lax.axis_size("z")
    piece = columns * own

    def to_owners(value, extras=(), extra_outs=(), beside=None):
        (out,) = call(
            lambda *refs: half_sum_kernel(own, False, *refs), [((half, width), bf16)],
            (live, value), flops=big // 2, name="half_away",
        )
        away = lax.ppermute(out, "core", swap)
        here = call(
            (lambda *refs: half_first_kernel(own, *refs))
            if extras
            else (lambda *refs: half_sum_kernel(own, True, *refs)),
            [((half, width), f32)] + list(extra_outs),
            (live, value) + tuple(extras), flops=big // 2, name="half_here",
        )
        sums = call(
            pieces_kernel,
            [((piece, width), bf16 if shift else f32) for shift in SHIFTS],
            (here[0], away), name="pieces",
        )
        got = [
            lax.ppermute(total, "y", ring(lanes, shift)) if shift else total
            for shift, total in zip(SHIFTS, sums)
        ]
        done = ()
        if beside is not None:
            got[-1], *done = lax.optimization_barrier((got[-1], *beside()))
        (both,) = call(total_kernel, [((columns, own, width), bf16)], got, name="total")
        parts = lax.all_to_all(both, "z", 0, 0, tiled=True)
        return (parts,) + tuple(here[1:]) + tuple(done)

    parts, own_cot = to_owners(normed, (mesh_cotangent,), (((own, width), bf16),))
    grad_copies, node_normed, d_pre = call(
        node_kernel,
        [((owners, own, width), bf16), ((own, width), f32), ((own, width), bf16)],
        (parts, own_mesh, own_cot, node_first, node_second, gains),
        flops=2 * own * width * width * 7,
        name="node",
    )
    near = lax.all_to_all(grad_copies, zy, 0, 0, tiled=True).reshape(half, width)
    far = lax.ppermute(near, "core", swap)
    (near_rows,) = call(
        lambda *refs: near_rows_kernel(own, *refs), [((edges, width), bf16)],
        (live, near), flops=big // 2, name="near_rows",
    )
    (d_first,) = call(
        lambda *refs: edge_backward_kernel(own, *refs),
        [((edges, width), bf16)],
        (
            live, near_rows, far, normed, slope, edge_second,
        ),
        scratch=[vm((edges, width), f32)],
        flops=big // 2 + dense,
        name="edge_backward",
    )
    def other_work():
        slots = call(
            slot_sum_kernel, [((side, width), bf16)] * 3, (send, d_first, edge_first),
            flops=dense, name="slot_sum",
        )
        grads = call(
            edge_grad_kernel, [((edges, width), bf16)], (d_first, edge_first),
            flops=dense, name="edge_grad",
        )
        late_normed, late_d_pre, _ = lax.optimization_barrier((node_normed, d_pre, d_first))
        node_outs = call(
            mesh_out_kernel,
            [((own, width), bf16), ((own, width), f32)],
            (own_mesh, own_cot, late_normed, late_d_pre, node_first, gains),
            flops=2 * own * width * width, name="mesh_out",
        )
        return (*slots, *grads, *node_outs)

    mesh_parts, back_low, back_own, back_high, edge_grad, mesh_out, direct = to_owners(
        d_first, beside=other_work
    )
    got_low = lax.ppermute(back_high, "lon", ring(lon_count, 1))
    got_high = lax.ppermute(back_low, "lon", ring(lon_count, -1))
    (grid_grad,) = call(
        grid_grad_kernel,
        [((grid_rows, width), bf16)],
        (send_rows, got_low, back_own, got_high),
        flops=2 * listed * grid_rows * width,
        name="grid_grad",
    )
    (mesh_grad,) = call(
        mesh_grad_kernel, [((own, width), bf16)], (mesh_parts, direct, edge_first), name="mesh_grad"
    )
    return (mesh_out, grid_grad, mesh_grad, edge_grad)


def solution(mesh):
    fine = Mesh(mesh.devices.reshape(mesh.shape["lon"], 8, 4, 2), ("lon", "z", "y", "core"))
    every = ("lon", "z", "y", "core")
    rows = P(every, None)
    flat = P(every)
    patch = P("lon", None)
    return jax.shard_map(
        shards,
        mesh=fine,
        in_specs=(rows, patch, rows, patch, flat, flat, rows, flat) + (P(),) * 6,
        out_specs=(rows, rows, rows, rows),
        check_vma=False,
    )
```

```python
import jax
import jax.numpy as jnp
from jax import lax
from jax.experimental import pallas as pl
from jax.experimental.pallas import tpu as pltpu
from jax.sharding import Mesh
from jax.sharding import PartitionSpec as P

eps = 1e-05
f32 = jnp.float32
bf16 = jnp.bfloat16
i32 = jnp.int32

LANES = 128
CHUNK = 256
MIB = 1 << 20


def dot(a, b):
    return lax.dot_general(a, b, (((1,), (0,)), ((), ())), preferred_element_type=f32)


def dot_nt(a, b):
    return lax.dot_general(a, b, (((1,), (1,)), ((), ())), preferred_element_type=f32)


def dot_tn(a, b):
    return lax.dot_general(a, b, (((0,), (0,)), ((), ())), preferred_element_type=f32)


def split_dot_nt(a, b):
    high = a.astype(bf16)
    low = (a - high.astype(f32)).astype(bf16)
    return dot_nt(high, b) + dot_nt(low, b)


def one_hot(mask):
    return jnp.where(mask, 1.0, 0.0).astype(bf16)


def call(kernel, outs, args, smem=(), hbm=(), scratch=(), limit=16, flops=0, name=None):
    def space(i):
        if i in smem:
            return pltpu.SMEM
        return pltpu.HBM if i in hbm else pltpu.VMEM

    return pl.pallas_call(
        kernel,
        out_shape=[jax.ShapeDtypeStruct(s, d) for s, d in outs],
        in_specs=[pl.BlockSpec(memory_space=space(i)) for i in range(len(args))],
        out_specs=[pl.BlockSpec(memory_space=pltpu.VMEM) for _ in outs],
        scratch_shapes=list(scratch),
        compiler_params=pltpu.CompilerParams(vmem_limit_bytes=limit * MIB),
        cost_estimate=pl.CostEstimate(flops=flops, bytes_accessed=0, transcendentals=0),
        name=name,
    )(*args)


def column(cols, start, size):
    parts = [cols[:, j : j + 1] for j in range(start // LANES, (start + size) // LANES)]
    return parts[0] if len(parts) == 1 else jnp.concatenate(parts, axis=0)


def row_hot(spot, rows, start, size):
    parts = [one_hot(spot == rows[j : j + 1, :]) for j in range(start // LANES, (start + size) // LANES)]
    return jnp.concatenate(parts, axis=1)


def chunks(rows, size):
    return [(at, slice(at, at + size)) for at in range(0, rows, size)]


def live_rows(rows_ref, count):
    rows = rows_ref[...]
    slot = lax.broadcasted_iota(i32, rows.shape, 0) * LANES + lax.broadcasted_iota(
        i32, rows.shape, 1
    )
    return jnp.where(slot < count, rows, -1)


def row_index_kernel(out_ref):
    out_ref[...] = lax.broadcasted_iota(i32, out_ref.shape, 0)


def halo_rows_kernel(
    index_ref, list_ref, grid_ref, count_ref, recv_ref, node_gain_ref, edge_gain_ref,
    low_ref, own_ref, high_ref, live_ref, gains_ref,
):
    gains_ref[0:1, :] = node_gain_ref[...]
    gains_ref[1:2, :] = edge_gain_ref[...]
    rows = dot_tn(one_hot(index_ref[...] == list_ref[...]), grid_ref[...]).astype(bf16)
    side = rows.shape[0] // 3
    low_ref[...] = rows[0:side]
    own_ref[...] = rows[side : 2 * side]
    high_ref[...] = rows[2 * side :]
    live_ref[...] = live_rows(recv_ref, count_ref[...])


def mesh_rows_kernel(live_ref, mesh_ref, out_ref, own_ref):
    own = own_ref.shape[0]
    own_ref[...] = mesh_ref[pl.ds(pl.multiple_of(my_block() * own, own), own), :]
    m = mesh_ref.shape[0]
    cols = jnp.transpose(live_ref[...])
    for start, at in chunks(out_ref.shape[0], LANES):
        hot = one_hot(lax.broadcasted_iota(i32, (LANES, m), 1) == column(cols, start, LANES))
        out_ref[at, :] = dot(hot, mesh_ref[...]).astype(bf16)


def edge_forward_kernel(
    send_ref, edge_ref, mesh_rows_ref, low_ref, own_ref, high_ref, first_ref, second_ref,
    normed_ref, slope_ref, work_ref, post_ref,
):
    listed = jnp.concatenate([low_ref[...], own_ref[...], high_ref[...]], axis=0)
    n = listed.shape[0]
    cols = jnp.transpose(send_ref[...])
    parts = chunks(edge_ref.shape[0], CHUNK)
    for start, at in parts:
        hot = one_hot(lax.broadcasted_iota(i32, (CHUNK, n), 1) == column(cols, start, CHUNK))
        source = dot(hot, listed).astype(bf16)
        given = jnp.concatenate([edge_ref[at, :], source, mesh_rows_ref[at, :]], axis=1)
        work_ref[at, :] = dot(given, first_ref[...])
    for _, at in parts:
        first = work_ref[at, :]
        sigma = jax.nn.sigmoid(first)
        act = first * sigma
        work_ref[at, :] = sigma + act * (1.0 - sigma)
        post_ref[at, :] = dot(act.astype(bf16), second_ref[...])
    for _, at in parts:
        normed, factor = norm(post_ref[at, :])
        normed_ref[at, :] = normed.astype(bf16)
        slope_ref[at, :] = (factor * work_ref[at, :]).astype(bf16)


def my_core():
    return lax.axis_index("core").astype(i32)


def my_block():
    return (lax.axis_index("z") * 8 + lax.axis_index("y") * 2 + lax.axis_index("core")).astype(i32)


def my_lane(shift):
    return lax.rem(lax.axis_index("y").astype(i32) + shift, lax.axis_size("y"))


def block_sum(own, y, core, live, value_ref):
    lanes = lax.axis_size("y")
    i = lax.broadcasted_iota(i32, (own * lax.axis_size("z"), LANES), 0)
    spot = (i // own) * (2 * lanes * own) + (2 * y + core) * own + i % own
    total = jnp.zeros((spot.shape[0], value_ref.shape[1]), f32)
    for begin, at in chunks(value_ref.shape[0], CHUNK):
        total = total + dot(row_hot(spot, live, begin, CHUNK), value_ref[at, :])
    return total


SHIFTS = (1, 3, 2, 0)


def half_sum_kernel(own, here, live_ref, value_ref, out_ref):
    live = live_ref[...]
    core = my_core() if here else 1 - my_core()
    size = out_ref.shape[0] // len(SHIFTS)
    for n, shift in enumerate(SHIFTS):
        total = block_sum(own, my_lane(shift), core, live, value_ref)
        out_ref[n * size : (n + 1) * size, :] = total.astype(out_ref.dtype)


def half_first_kernel(own, live_ref, value_ref, cot_ref, out_ref, own_cot_ref):
    half_sum_kernel(own, True, live_ref, value_ref, out_ref)
    own_cot_ref[...] = cot_ref[pl.ds(pl.multiple_of(my_block() * own, own), own), :]


def pieces_kernel(here_ref, away_ref, *out_refs):
    size = here_ref.shape[0] // len(out_refs)
    for n, out_ref in enumerate(out_refs):
        at = slice(n * size, (n + 1) * size)
        out_ref[...] = (here_ref[at, :] + away_ref[at, :].astype(f32)).astype(out_ref.dtype)


def total_kernel(a_ref, b_ref, c_ref, here_ref, out_ref):
    far = a_ref[...].astype(f32) + (b_ref[...].astype(f32) + c_ref[...].astype(f32))
    out_ref[...] = (here_ref[...] + far).astype(bf16).reshape(out_ref.shape)


def norm(value):
    center = value - jnp.mean(value, axis=-1, keepdims=True)
    factor = lax.rsqrt(jnp.mean(center * center, axis=-1, keepdims=True) + eps)
    return center * factor, factor


def node_kernel(
    parts_ref, mesh_ref, cot_ref, first_ref, second_ref, gains_ref, grad_ref, normed_ref, d_pre_ref,
):
    width = mesh_ref.shape[1]
    aggregate = jnp.sum(parts_ref[...].astype(f32), axis=0)
    agg_low = (aggregate * gains_ref[1:2, :]).astype(bf16)
    mesh = mesh_ref[...]
    gain = gains_ref[0:1, :]
    pre = dot(mesh, first_ref[0:width, :]) + dot(agg_low, first_ref[width : 2 * width, :])
    sigma = jax.nn.sigmoid(pre)
    act = (pre * sigma).astype(bf16)
    post = dot(act, second_ref[...])
    normed, factor = norm(post)
    normed_ref[...] = normed
    scaled = cot_ref[...].astype(f32) * gain
    d_post = factor * (
        scaled
        - jnp.mean(scaled, axis=-1, keepdims=True)
        - normed * jnp.mean(scaled * normed, axis=-1, keepdims=True)
    )
    d_pre = dot_nt(d_post.astype(bf16), second_ref[...]) * (sigma * (1.0 + pre * (1.0 - sigma)))
    d_pre = d_pre.astype(bf16)
    grad = dot_nt(d_pre, first_ref[width : 2 * width, :]).astype(bf16)
    grad_ref[...] = jnp.broadcast_to(grad[None], grad_ref.shape)
    d_pre_ref[...] = d_pre


def mesh_out_kernel(
    mesh_ref, cot_ref, normed_ref, d_pre_ref, first_ref, gains_ref, out_ref, direct_ref
):
    width = mesh_ref.shape[1]
    out_ref[...] = (mesh_ref[...].astype(f32) + normed_ref[...] * gains_ref[0:1, :]).astype(bf16)
    direct_ref[...] = cot_ref[...].astype(f32) + dot_nt(d_pre_ref[...], first_ref[0:width, :])


def half_place(own, core, live):
    place = (live // (2 * own)) * own + live % own
    return jnp.where((live // own) % 2 == core, place, -1)


def near_rows_kernel(own, live_ref, near_ref, out_ref):
    half = near_ref.shape[0]
    place = half_place(own, my_core(), live_ref[...])
    cols = jnp.transpose(place)
    for start, at in chunks(out_ref.shape[0], LANES):
        hot = one_hot(lax.broadcasted_iota(i32, (LANES, half), 1) == column(cols, start, LANES))
        out_ref[at, :] = dot(hot, near_ref[...]).astype(bf16)


def edge_backward_kernel(
    own, live_ref, near_rows_ref, far_ref, normed_ref, slope_ref, second_ref,
    gains_ref, out_ref, work_ref,
):
    half = far_ref.shape[0]
    place = half_place(own, 1 - my_core(), live_ref[...])
    cols = jnp.transpose(place)
    for start, at in chunks(out_ref.shape[0], LANES):
        hot = one_hot(lax.broadcasted_iota(i32, (LANES, half), 1) == column(cols, start, LANES))
        work_ref[at, :] = dot(hot, far_ref[...]) + near_rows_ref[at, :].astype(f32)
    gain = gains_ref[1:2, :]
    for _, at in chunks(out_ref.shape[0], CHUNK):
        scaled = work_ref[at, :] * gain
        normed = normed_ref[at, :].astype(f32)
        inner = (
            scaled
            - jnp.mean(scaled, axis=-1, keepdims=True)
            - normed * jnp.mean(scaled * normed, axis=-1, keepdims=True)
        ).astype(bf16)
        out_ref[at, :] = (dot_nt(inner, second_ref[...]) * slope_ref[at, :].astype(f32)).astype(bf16)


def slot_sum_kernel(send_ref, d_first_ref, first_ref, low_ref, own_ref, high_ref):
    width = d_first_ref.shape[1]
    side = low_ref.shape[0]
    spot = lax.broadcasted_iota(i32, (3 * side, LANES), 0)
    total = jnp.zeros((3 * side, width), f32)
    for start, at in chunks(d_first_ref.shape[0], CHUNK):
        total = total + dot(row_hot(spot, send_ref, start, CHUNK), d_first_ref[at, :])
    terms = split_dot_nt(total, first_ref[width : 2 * width, :]).astype(bf16)
    low_ref[...] = terms[0:side]
    own_ref[...] = terms[side : 2 * side]
    high_ref[...] = terms[2 * side :]


def edge_grad_kernel(d_first_ref, first_ref, out_ref):
    width = d_first_ref.shape[1]
    for i in range(out_ref.shape[0] // CHUNK):
        at = slice(i * CHUNK, (i + 1) * CHUNK)
        out_ref[at, :] = dot_nt(d_first_ref[at, :], first_ref[0:width, :]).astype(bf16)


def grid_grad_kernel(list_ref, low_ref, own_ref, high_ref, out_ref):
    terms = jnp.concatenate([low_ref[...], own_ref[...], high_ref[...]], axis=0)
    spot = lax.broadcasted_iota(i32, (out_ref.shape[0], terms.shape[0]), 0)
    out_ref[...] = dot(one_hot(spot == list_ref[...]), terms).astype(bf16)


def mesh_grad_kernel(parts_ref, direct_ref, first_ref, out_ref):
    width = direct_ref.shape[1]
    total = jnp.sum(parts_ref[...].astype(f32), axis=0)
    out_ref[...] = (
        direct_ref[...] + split_dot_nt(total, first_ref[2 * width : 3 * width, :])
    ).astype(bf16)


def ring(count, shift):
    return [(i, (i + shift) % count) for i in range(count)]


def shards(
    grid_latent,
    mesh_latent,
    edge_latent,
    mesh_cotangent,
    edge_senders,
    edge_receivers,
    send_rows,
    edge_count,
    edge_first,
    edge_second,
    edge_gain,
    node_first,
    node_second,
    node_gain,
):
    width = grid_latent.shape[1]
    zy = ("z", "y")
    lon_count = lax.axis_size("lon")
    owners = lax.axis_size("z") * lax.axis_size("y")
    listed = send_rows.shape[1]
    side = listed // 3
    patch = mesh_latent.shape[0]
    own = patch // (2 * owners)
    half = patch // 2
    edges = edge_latent.shape[0]
    grid_rows = grid_latent.shape[0]
    recv = edge_receivers.reshape(edges // LANES, LANES)
    send = edge_senders.reshape(edges // LANES, LANES)
    swap = [(0, 1), (1, 0)]
    big = 2 * edges * patch * width
    dense = 2 * edges * width * width

    vm = pltpu.VMEM
    (index,) = call(
        row_index_kernel, [((grid_rows, listed), i32)], (), flops=2 * big, name="row_index"
    )
    to_low, stay, to_high, live, gains = call(
        halo_rows_kernel,
        [((side, width), bf16)] * 3 + [(recv.shape, i32), ((2, width), f32)],
        (
            index, send_rows, grid_latent, edge_count.reshape(1, 1), recv,
            node_gain.reshape(1, width), edge_gain.reshape(1, width),
        ),
        flops=2 * big,
        name="halo_rows",
    )
    from_low = lax.ppermute(to_high, "lon", ring(lon_count, 1))
    from_high = lax.ppermute(to_low, "lon", ring(lon_count, -1))
    mesh_rows, own_mesh = call(
        mesh_rows_kernel,
        [((edges, width), bf16), ((own, width), bf16)],
        (live, mesh_latent),
        flops=big,
        name="mesh_rows",
    )
    normed, slope = call(
        edge_forward_kernel,
        [((edges, width), bf16)] * 2,
        (send, edge_latent, mesh_rows, from_low, stay, from_high, edge_first, edge_second),
        scratch=[vm((edges, width), f32)] * 2,
        flops=5 * dense,
        name="edge_forward",
    )

    lanes = lax.axis_size("y")
    columns = lax.axis_size("z")
    piece = columns * own

    def to_owners(value, extras=(), extra_outs=(), beside=None):
        (out,) = call(
            lambda *refs: half_sum_kernel(own, False, *refs), [((half, width), bf16)],
            (live, value), flops=big // 2, name="half_away",
        )
        away = lax.ppermute(out, "core", swap)
        here = call(
            (lambda *refs: half_first_kernel(own, *refs))
            if extras
            else (lambda *refs: half_sum_kernel(own, True, *refs)),
            [((half, width), f32)] + list(extra_outs),
            (live, value) + tuple(extras), flops=big // 2, name="half_here",
        )
        sums = call(
            pieces_kernel,
            [((piece, width), bf16 if shift else f32) for shift in SHIFTS],
            (here[0], away), name="pieces",
        )
        got = [
            lax.ppermute(total, "y", ring(lanes, shift)) if shift else total
            for shift, total in zip(SHIFTS, sums)
        ]
        done = ()
        if beside is not None:
            got[-1], *done = lax.optimization_barrier((got[-1], *beside()))
        (both,) = call(total_kernel, [((columns, own, width), bf16)], got, name="total")
        parts = lax.all_to_all(both, "z", 0, 0, tiled=True)
        return (parts,) + tuple(here[1:]) + tuple(done)

    parts, own_cot = to_owners(normed, (mesh_cotangent,), (((own, width), bf16),))
    grad_copies, node_normed, d_pre = call(
        node_kernel,
        [((owners, own, width), bf16), ((own, width), f32), ((own, width), bf16)],
        (parts, own_mesh, own_cot, node_first, node_second, gains),
        flops=2 * own * width * width * 7,
        name="node",
    )
    near = lax.all_to_all(grad_copies, zy, 0, 0, tiled=True).reshape(half, width)
    far = lax.ppermute(near, "core", swap)
    (near_rows,) = call(
        lambda *refs: near_rows_kernel(own, *refs), [((edges, width), bf16)],
        (live, near), flops=big // 2, name="near_rows",
    )
    (d_first,) = call(
        lambda *refs: edge_backward_kernel(own, *refs),
        [((edges, width), bf16)],
        (
            live, near_rows, far, normed, slope, edge_second,
            gains,
        ),
        scratch=[vm((edges, width), f32)],
        flops=big // 2 + dense,
        name="edge_backward",
    )
    def other_work():
        slots = call(
            slot_sum_kernel, [((side, width), bf16)] * 3, (send, d_first, edge_first),
            flops=dense, name="slot_sum",
        )
        late_normed, late_d_pre, _ = lax.optimization_barrier((node_normed, d_pre, d_first))
        node_outs = call(
            mesh_out_kernel,
            [((own, width), bf16), ((own, width), f32)],
            (own_mesh, own_cot, late_normed, late_d_pre, node_first, gains),
            flops=2 * own * width * width, name="mesh_out",
        )
        return (*slots, *node_outs)

    mesh_parts, back_low, back_own, back_high, mesh_out, direct = to_owners(
        d_first, beside=other_work
    )
    got_low = lax.ppermute(back_high, "lon", ring(lon_count, 1))
    got_high = lax.ppermute(back_low, "lon", ring(lon_count, -1))
    late_first, _ = lax.optimization_barrier((d_first, back_own))
    (edge_grad,) = call(
        edge_grad_kernel, [((edges, width), bf16)], (late_first, edge_first),
        flops=dense, name="edge_grad",
    )
    (grid_grad,) = call(
        grid_grad_kernel,
        [((grid_rows, width), bf16)],
        (send_rows, got_low, back_own, got_high),
        flops=2 * listed * grid_rows * width,
        name="grid_grad",
    )
    (mesh_grad,) = call(
        mesh_grad_kernel, [((own, width), bf16)], (mesh_parts, direct, edge_first), name="mesh_grad"
    )
    return (mesh_out, grid_grad, mesh_grad, edge_grad)


def solution(mesh):
    fine = Mesh(mesh.devices.reshape(mesh.shape["lon"], 8, 4, 2), ("lon", "z", "y", "core"))
    every = ("lon", "z", "y", "core")
    rows = P(every, None)
    flat = P(every)
    patch = P("lon", None)
    return jax.shard_map(
        shards,
        mesh=fine,
        in_specs=(rows, patch, rows, patch, flat, flat, rows, flat) + (P(),) * 6,
        out_specs=(rows, rows, rows, rows),
        check_vma=False,
    )
```
